128 devices in a mesh: seg: 8 (over y, x_lo), grp: 16 (over x_hi, z, core).
Axes of the slice: x: 4 (x_hi: 2, x_lo: 2; x = x_hi * 2 + x_lo), y: 4, z: 4, core: 2. Of those that a mesh axis runs over, the one named last changes fastest.
Arguments:
- tile_tokens: bfloat16 [131072, 1536], P(('seg', 'grp')), may hold values from -6 to 6
- gate_weight: bfloat16 [1536, 2048], P(('seg', 'grp')), may hold values from -0.15625 to 0.15625
- up_weight: bfloat16 [1536, 2048], P(('seg', 'grp')), may hold values from -0.15625 to 0.15625
- down_weight: bfloat16 [2048, 1536], P(('seg', 'grp')), may hold values from -0.125 to 0.125
- proj_weight: bfloat16 [1536, 768], replicated, may hold values from -0.15625 to 0.15625
- query_weight: bfloat16 [768, 768], replicated, may hold values from -40 to 40
- key_weight: bfloat16 [768, 768], replicated, may hold values from -1 to 1
- value_weight: bfloat16 [768, 768], replicated, may hold values from -0.21875 to 0.21875
- tile_rank: int32 [131072], P(('seg', 'grp')), may hold values from 0 to 131071, as said below
- valid_count: int32 [1], replicated, may hold values from 65536 to 131071
Outputs:
- attended: bfloat16 [16, 8192, 768], P('grp', 'seg')
The draws below stay inside these ranges and needn't reach their ends.
Inputs may be any that keep to these rules, and one draw needn't show every extreme that they name: `tile_rank`: A permutation of the positions. Device with seg index s and grp index g holds tiles 1024 * (s * (number of grp devices) + g) onward and positions 8192 * g + 1024 * s onward. At most 16 tiles of one device's batch take positions in one device's block, exactly 16 for some pairs in every draw; that number depends only on the difference of the two devices' flat indices modulo the number of devices.
All inputs are finite; a program needn't handle non-finite values.
Results may differ from the reference program's by a relative error of at most 0.028.
Values may be sent and summed in bfloat16 or wider, within the bound.
No kernel may reach another device: no remote copies, remote signals or barrier semaphores. Data moves between devices by JAX's collectives and lax.ppermute only.
A program may use at most 192 MiB of HBM per device.

```python
import math
import jax
import jax.numpy as jnp
from jax import lax

D_VIT = 1536
FF = 2048
D = 768
HEADS = 16
LOC = 512
RATE = 4
TOK_DEV = 1024
TILES = 131072
SEG_TOK = 8192
CAP = 16
N_SEG = 8
N_GRP = 16


def key_matrix(key):
    base = jax.random.fold_in(key, 11)
    return jnp.clip(jax.random.normal(base, (D, D), jnp.float32), -5.0, 5.0) / math.sqrt(D)


def draw_key_weight(key, part):
    shared = key_matrix(key)
    return shared.astype(jnp.bfloat16)


def draw_query_weight(key, part):
    key = jax.random.fold_in(key, 2)
    own = jnp.clip(jax.random.normal(key, (D, D), jnp.float32), -5.0, 5.0) * (3.0 / math.sqrt(D))
    return own.astype(jnp.bfloat16)


def draw_tile_rank(key, part):
    key = jax.random.fold_in(key, 3)
    devices = N_SEG * N_GRP
    cell_count = devices * CAP
    favored = jax.random.randint(jax.random.fold_in(key, 1), (), 0, devices)
    cell_offset = jnp.arange(cell_count, dtype=jnp.int32) // CAP
    shuffled = jax.random.permutation(jax.random.fold_in(key, 2), cell_count).astype(jnp.int32)
    cell_score = jnp.where(cell_offset == favored, 0, cell_count) + shuffled
    cell_rank = jnp.argsort(jnp.argsort(cell_score))
    chosen = cell_rank < TOK_DEV
    offset_count = jax.ops.segment_sum(chosen.astype(jnp.int32), cell_offset, num_segments=devices)
    group_end = jnp.cumsum(offset_count).astype(jnp.int32)
    bound_top = 2 ** 30 // TOK_DEV
    column_index = jnp.arange(TOK_DEV, dtype=jnp.int32)[None, :]
    source_keys = jax.random.randint(jax.random.fold_in(key, 3), (devices, TOK_DEV), 0, bound_top) * TOK_DEV + column_index
    slot_index = jnp.argsort(source_keys, axis=1).astype(jnp.int32)
    lag_index = jnp.searchsorted(group_end, slot_index, side='right').astype(jnp.int32)
    source_dev = jnp.arange(devices, dtype=jnp.int32)[:, None]
    target_dev = (source_dev - lag_index) % devices
    target_keys = jax.random.randint(jax.random.fold_in(key, 4), (devices, TOK_DEV), 0, bound_top) * TOK_DEV + column_index
    target_perm = jnp.argsort(target_keys, axis=1).astype(jnp.int32)
    within = target_perm[target_dev, slot_index]
    position = target_dev % N_GRP * (N_SEG * TOK_DEV) + target_dev // N_GRP * TOK_DEV + within
    return position.reshape(devices * TOK_DEV).astype(jnp.int32)


def block_levels(rng, extent, cuts, least, high):
    loudness = 1.0
    for dim, shards_of in cuts:
        steps = jax.random.uniform(jax.random.fold_in(jax.random.fold_in(rng, 6), dim), (shards_of,), jnp.float32, least / len(cuts), high / len(cuts))
        loudness = loudness * jnp.repeat(jnp.exp(steps), extent[dim] // shards_of).reshape((-1,) + (1,) * (len(extent) - 1 - dim))
    return loudness


def scatter_about(stream_key, shape, spread, most, split=(), kind=jnp.bfloat16):
    array = spread * jax.random.normal(stream_key, shape, jnp.float32)
    if split:
        array = array * block_levels(stream_key, shape, split, -0.22, 0.18)
    return jnp.clip(array, -most, most).astype(kind)


def setup_inputs(seed: int = 0) -> dict:
    arg_keys = jax.random.split(jax.random.key(seed), 11)
    return {
        "tile_tokens": scatter_about(arg_keys[0], (TILES, D_VIT), 1.0, 6.0, ((0, 128),)),
        "gate_weight": scatter_about(arg_keys[1], (D_VIT, FF), D_VIT ** -0.5, 0.15625, ((0, 128),)),
        "up_weight": scatter_about(arg_keys[2], (D_VIT, FF), D_VIT ** -0.5, 0.15625, ((0, 128),)),
        "down_weight": scatter_about(arg_keys[3], (FF, D_VIT), FF ** -0.5, 0.125, ((0, 128),)),
        "proj_weight": scatter_about(arg_keys[4], (D_VIT, D), D_VIT ** -0.5, 0.15625),
        "query_weight": draw_query_weight(jax.random.fold_in(arg_keys[10], 71), 0),
        "key_weight": draw_key_weight(jax.random.fold_in(arg_keys[10], 71), 0),
        "value_weight": scatter_about(arg_keys[7], (D, D), D ** -0.5, 0.21875),
        "tile_rank": draw_tile_rank(jax.random.fold_in(arg_keys[10], 71), 0),
        "valid_count": jax.random.randint(arg_keys[9], (1,), TILES // 2, TILES).astype(jnp.int32),
    }


def layer_norm(values, epsilon):
    row_mean = lax.optimization_barrier(jnp.mean(values, axis=-1, keepdims=True))
    centered = values - row_mean
    row_var = lax.optimization_barrier(jnp.mean(centered * centered, axis=-1, keepdims=True))
    return centered * lax.rsqrt(row_var + epsilon)

def diagonal_rows(values):
    length = values.shape[0]
    shaped = values.reshape(length // RATE, RATE, HEADS // RATE, RATE, D // HEADS)
    picked = jnp.diagonal(shaped, axis1=1, axis2=3)
    return jnp.transpose(picked, (0, 1, 3, 2)).reshape(length // RATE, D)

def reference(tile_tokens, gate_weight, up_weight, down_weight, proj_weight, query_weight, key_weight, value_weight, tile_rank, valid_count):

    def tile_block(block):
        residual = block.astype(jnp.float32)
        normed = layer_norm(residual, 1e-06).astype(jnp.bfloat16)
        gate_acc = jnp.dot(normed, gate_weight, preferred_element_type=jnp.float32)
        up_acc = jnp.dot(normed, up_weight, preferred_element_type=jnp.float32)
        hidden = (jax.nn.silu(gate_acc) * up_acc).astype(jnp.bfloat16)
        mixed = residual + jnp.dot(hidden, down_weight, preferred_element_type=jnp.float32)
        final_normed = layer_norm(mixed, 1e-06).astype(jnp.bfloat16)
        return jnp.dot(final_normed, proj_weight, preferred_element_type=jnp.float32).astype(jnp.bfloat16)
    embedded = lax.map(tile_block, tile_tokens.reshape(TILES // TOK_DEV, TOK_DEV, D_VIT)).reshape(TILES, D)
    sequence = jnp.zeros((TILES, D), jnp.bfloat16).at[tile_rank.astype(jnp.int32)].set(embedded)
    live_mask = jnp.arange(TILES, dtype=jnp.int32) < valid_count[0].astype(jnp.int32)
    normed_seq = layer_norm(sequence.astype(jnp.float32), 1e-05).astype(jnp.bfloat16)
    query_rows = jnp.dot(normed_seq, query_weight, preferred_element_type=jnp.float32).astype(jnp.bfloat16)
    key_rows = jnp.dot(normed_seq, key_weight, preferred_element_type=jnp.float32).astype(jnp.bfloat16)
    value_rows = jnp.dot(normed_seq, value_weight, preferred_element_type=jnp.float32).astype(jnp.bfloat16)
    head_size = D // HEADS
    score_scale = 1.0 / math.sqrt(head_size)

    def local_branch(operands):
        query_blk, key_blk, value_blk, keep_blk = operands
        scores = jnp.einsum('qhd,khd->hqk', query_blk.astype(jnp.float32), key_blk.astype(jnp.float32), precision=lax.Precision.HIGHEST) * score_scale
        allowed = keep_blk[None, None, :] | jnp.eye(LOC, dtype=jnp.bool_)[None]
        scores = jnp.where(allowed, scores, -jnp.inf)
        row_max = lax.optimization_barrier(jnp.max(scores, axis=-1))
        weights = jnp.exp(scores - row_max[..., None])
        row_total = lax.optimization_barrier(jnp.sum(weights, axis=-1))
        rounded = lax.optimization_barrier(weights.astype(jnp.bfloat16)).astype(jnp.float32)
        accum = jnp.einsum('hqk,khd->qhd', rounded, value_blk.astype(jnp.float32), precision=lax.Precision.HIGHEST)
        return (row_max.T, row_total.T, accum)
    block_count = TILES // LOC
    near_max, near_total, near_acc = lax.map(local_branch, (query_rows.reshape(block_count, LOC, HEADS, head_size), key_rows.reshape(block_count, LOC, HEADS, head_size), value_rows.reshape(block_count, LOC, HEADS, head_size), live_mask.reshape(block_count, LOC)))
    sparse_len = SEG_TOK // RATE
    group_count = HEADS // RATE

    def dilated_branch(operands):
        query_seg, key_seg, value_seg, keep_seg = operands
        query_sp = diagonal_rows(query_seg).reshape(sparse_len, HEADS, head_size)
        key_sp = diagonal_rows(key_seg).reshape(sparse_len, HEADS, head_size)
        value_sp = diagonal_rows(value_seg).reshape(sparse_len, HEADS, head_size)
        keep_sp = jnp.tile(keep_seg.reshape(sparse_len, RATE), (1, group_count))
        scores = jnp.einsum('qhd,khd->hqk', query_sp.astype(jnp.float32), key_sp.astype(jnp.float32), precision=lax.Precision.HIGHEST) * score_scale
        allowed = keep_sp.T[:, None, :] | jnp.eye(sparse_len, dtype=jnp.bool_)[None]
        scores = jnp.where(allowed, scores, -jnp.inf)
        row_max = lax.optimization_barrier(jnp.max(scores, axis=-1))
        weights = jnp.exp(scores - row_max[..., None])
        row_total = lax.optimization_barrier(jnp.sum(weights, axis=-1))
        accum = jnp.einsum('hqk,khd->qhd', weights, value_sp.astype(jnp.float32), precision=lax.Precision.HIGHEST)
        return (row_max.T, row_total.T, accum)
    segment_count = TILES // SEG_TOK
    far_max, far_total, far_acc = lax.map(dilated_branch, (query_rows.reshape(segment_count, SEG_TOK, D), key_rows.reshape(segment_count, SEG_TOK, D), value_rows.reshape(segment_count, SEG_TOK, D), live_mask.reshape(segment_count, SEG_TOK)))
    near_shape = (TILES // RATE, RATE, group_count, RATE)
    far_shape = (TILES // RATE, 1, group_count, RATE)
    near_max = near_max.reshape(near_shape)
    near_total = near_total.reshape(near_shape)
    near_acc = near_acc.reshape(near_shape + (head_size,))
    far_max = far_max.reshape(far_shape)
    far_total = far_total.reshape(far_shape)
    far_acc = far_acc.reshape(far_shape + (head_size,))
    same_phase = jnp.eye(RATE, dtype=jnp.bool_)[:, None, :]
    best_max = jnp.where(same_phase, jnp.maximum(near_max, far_max), near_max)
    near_coef = jnp.exp(near_max - best_max)
    far_coef = jnp.where(same_phase, jnp.exp(jnp.where(same_phase, far_max - best_max, 0.0)), 0.0)
    numerator = near_coef[..., None] * near_acc + far_coef[..., None] * far_acc
    denominator = near_coef * near_total + far_coef * far_total
    attended = (numerator / denominator[..., None]).reshape(TILES, D)
    attended = jnp.where(live_mask[:, None], attended, 0.0).astype(jnp.bfloat16)
    return attended.reshape(segment_count, SEG_TOK, D)
```

```python
import functools
import math

import jax
import jax.numpy as jnp
from jax import lax
from jax.experimental import pallas as pl
from jax.experimental.pallas import tpu as pltpu
from jax.sharding import PartitionSpec as P

D = 768
DV = 1536
FF = 2048
HEADS = 16
LOC = 512
RATE = 4
HS = 48
HP = 64
CAP = 16
ALL = ("seg", "grp")
SIDE = 4
REL = (0, 1, 2, -1)
QSCALE = 1.4426950408889634 / math.sqrt(HS)
NEG = -1e30
F32 = jnp.float32
BF16 = jnp.bfloat16
VMEM_BYTES = 56 * 1024 * 1024


def flat_of(x, y, z, core):
    return (y * 2 + x % 2) * 16 + (x // 2) * 8 + z * 2 + core


def device_pairs(move):
    pairs = []
    for x in range(SIDE):
        for y in range(SIDE):
            for z in range(SIDE):
                for core in range(2):
                    there = move(x, y, z, core)
                    there = tuple(v % SIDE for v in there[:3]) + (there[3],)
                    pairs.append((flat_of(x, y, z, core), flat_of(*there)))
    return pairs


def shifted(axis, by):
    def move(x, y, z, core):
        at = [x, y, z]
        at[axis] += by
        return (*at, core)

    return device_pairs(move)


def ring_step(axis):
    def move(x, y, z, core):
        at = [x, y, z]
        at[axis] += 1 - 2 * core
        return (*at, core)

    return device_pairs(move)


def sent(value, pairs):
    return lax.ppermute(value, ALL, pairs)


def to_other_core(value):
    return sent(value, device_pairs(lambda x, y, z, core: (x, y, z, 1 - core)))


def from_side(block, axis):
    return [block if off == 0 else sent(block, shifted(axis, -off)) for off in REL]


def params(**kw):
    return pltpu.CompilerParams(vmem_limit_bytes=VMEM_BYTES, **kw)


def iota(shape, dim):
    return lax.broadcasted_iota(jnp.int32, shape, dim)


def dot(left, right):
    return jnp.dot(left, right, preferred_element_type=F32)


def dot_t(left, right):
    return lax.dot_general(left, right, (((1,), (1,)), ((), ())), preferred_element_type=F32)


def layer_norm(values, epsilon):
    row_mean = jnp.mean(values, axis=-1, keepdims=True)
    centered = values - row_mean
    row_var = jnp.mean(centered * centered, axis=-1, keepdims=True)
    return centered * lax.rsqrt(row_var + epsilon)


def onehot(mask):
    return jnp.where(mask, 1.0, 0.0).astype(BF16)


def column_kernel(core_ref, gate_ref, up_ref, out_ref):
    core = core_ref[0]
    rows = jnp.concatenate([gate_ref[...].astype(F32), up_ref[...].astype(F32)], axis=0).astype(BF16)
    width = 256
    for start in range(0, FF, width):
        n = iota((FF, width), 1) + start
        unit = n & 15
        x = (n >> 4) & 3
        y = (n >> 6) & 3
        z = (n >> 8) & 3
        half = (n >> 10) ^ core
        source = ((y * 2 + (x & 1)) * 16 + (x >> 1) * 8 + z * 2 + half) * 16 + unit
        picked = dot(rows, onehot(iota((FF, width), 0) == source)).astype(BF16)
        out_ref[start // 1024, :, start % 1024 : start % 1024 + width] = picked


def arrange_columns(core, gate, up):
    return pl.pallas_call(
        column_kernel,
        out_shape=jax.ShapeDtypeStruct((2, 24, FF // 2), BF16),
        in_specs=[
            pl.BlockSpec(memory_space=pltpu.SMEM),
            pl.BlockSpec(memory_space=pltpu.VMEM),
            pl.BlockSpec(memory_space=pltpu.VMEM),
        ],
        out_specs=pl.BlockSpec(memory_space=pltpu.VMEM),
        compiler_params=params(),
    )(core, gate, up)


def norm_kernel(order_ref, tokens_ref, out_ref, pick_ref):
    @pl.when(pl.program_id(0) == 0)
    def _():
        for which in range(2):
            for block in range(4):
                lanes = slice(block * 384, block * 384 + 384)
                pick_ref[which, block] = onehot(
                    iota((DV, 384), 0) == order_ref[which : which + 1, lanes]
                )

    normed = layer_norm(tokens_ref[...].astype(F32), 1e-06).astype(BF16)
    for which in range(2):
        for block in range(4):
            out_ref[which, block] = dot(normed, pick_ref[which, block]).astype(BF16)


def norm_tiles(order, tokens):
    rows = tokens.shape[0]
    tile = 256
    return pl.pallas_call(
        norm_kernel,
        grid=(rows // tile,),
        out_shape=jax.ShapeDtypeStruct((2, 4, rows, 384), BF16),
        in_specs=[
            pl.BlockSpec((2, DV), lambda i: (0, 0)),
            pl.BlockSpec((tile, DV), lambda i: (i, 0)),
        ],
        out_specs=pl.BlockSpec((2, 4, tile, 384), lambda i: (0, 0, i, 0)),
        scratch_shapes=[pltpu.VMEM((2, 4, DV, 384), BF16)],
        compiler_params=params(),
    )(order, tokens)


def ffn_kernel(block_ref, x_ref, *refs):
    gates, ups, downs = refs[0:4], refs[4:8], refs[8:12]
    out_ref, hid_ref = refs[12], refs[13]
    gate = up = None
    for t in range(4):
        g = dot(x_ref[0, block_ref[0, t]], gates[t][...])
        u = dot(x_ref[1, block_ref[1, t]], ups[t][...])
        gate = g if gate is None else gate + g
        up = u if up is None else up + u
    hidden = (gate / (1.0 + jnp.exp(-gate)) * up).astype(BF16)
    for block in range(4):
        hid_ref[block] = hidden[:, block * 256 : block * 256 + 256]
    total = None
    for t in range(4):
        part = dot(hid_ref[block_ref[2, t]], downs[t][...])
        total = part if total is None else total + part
    out_ref[...] = total.astype(out_ref.dtype)


def ffn(blocks, x, gates, ups, downs, dtype):
    rows = x.shape[2]
    tile = 256

    def whole(shape):
        return pl.BlockSpec(shape, lambda i: (0, 0))

    return pl.pallas_call(
        ffn_kernel,
        grid=(rows // tile,),
        out_shape=jax.ShapeDtypeStruct((rows, DV), dtype),
        in_specs=[
            pl.BlockSpec(memory_space=pltpu.SMEM),
            pl.BlockSpec((2, 4, tile, 384), lambda i: (0, 0, i, 0)),
        ]
        + [whole((384, 1024))] * 8
        + [whole((256, DV))] * 4,
        out_specs=pl.BlockSpec((tile, DV), lambda i: (i, 0)),
        scratch_shapes=[pltpu.VMEM((4, tile, 256), BF16)],
        compiler_params=params(),
        cost_estimate=pl.CostEstimate(
            flops=2 * rows * DV * 1024 * 3, bytes_accessed=20_000_000, transcendentals=rows * 1024
        ),
    )(blocks, x, *gates, *ups, *downs)


def slot_kernel(rank_ref, slot_ref, place_ref):
    rank = rank_ref[...]
    rows = rank.shape[1]
    devices = 128
    target = ((rank & 8191) >> 10) * 16 + (rank >> 13)
    within = rank & 1023
    hit = iota((devices, rows), 0) == target
    marks = onehot(hit)
    earlier = onehot(iota((rows, rows), 0) < iota((rows, rows), 1))
    before = dot(marks, earlier)
    number = jnp.sum(jnp.where(hit, before, 0.0), axis=0, keepdims=True)
    slot = target * CAP + number.astype(jnp.int32)
    slot_ref[...] = slot
    line = iota((8, rows), 0)
    place = ((within >> 9) << 9) + ((within & 3) << 7) + ((within >> 2) & 127)
    values = jnp.where(
        line == 0, place >> 5, jnp.where(line == 1, place & 31, jnp.where(line == 2, 1, 0))
    ).astype(F32).astype(BF16)
    for start in range(0, devices * CAP, 512):
        taken = onehot(iota((512, rows), 0) + start == slot)
        got = dot_t(values, taken)
        coded = got[0:1] * 32.0 + got[1:2] + got[2:3] - 1.0
        place_ref[:, start : start + 512] = coded.astype(jnp.int32)


def slots(rank):
    rows = rank.shape[0]
    return pl.pallas_call(
        slot_kernel,
        out_shape=(
            jax.ShapeDtypeStruct((1, rows), jnp.int32),
            jax.ShapeDtypeStruct((1, 128 * CAP), jnp.int32),
        ),
        compiler_params=params(),
    )(rank.reshape(1, rows))


def tail_kernel(slot_ref, tokens_ref, own_ref, other_ref, proj_ref, out_ref, emb_ref):
    step = pl.program_id(0)
    tile = tokens_ref.shape[0]
    mixed = tokens_ref[...].astype(F32) + own_ref[...] + other_ref[...].astype(F32)
    final = layer_norm(mixed, 1e-06).astype(BF16)
    emb_ref[pl.ds(pl.multiple_of(step * tile, tile), tile), :] = dot(final, proj_ref[...]).astype(BF16)

    @pl.when(step == pl.num_programs(0) - 1)
    def _():
        rows = emb_ref.shape[0]
        for start in range(0, out_ref.shape[0], 512):
            pick = onehot(iota((512, rows), 0) + start == slot_ref[...])
            out_ref[start : start + 512, :] = dot(pick, emb_ref[...]).astype(BF16)


def tail(slot, tokens, own, other, proj):
    rows = tokens.shape[0]
    tile = 256
    return pl.pallas_call(
        tail_kernel,
        grid=(rows // tile,),
        out_shape=jax.ShapeDtypeStruct((128 * CAP, D), BF16),
        in_specs=[
            pl.BlockSpec((1, rows), lambda i: (0, 0)),
            pl.BlockSpec((tile, DV), lambda i: (i, 0)),
            pl.BlockSpec((tile, DV), lambda i: (i, 0)),
            pl.BlockSpec((tile, DV), lambda i: (i, 0)),
            pl.BlockSpec((DV, D), lambda i: (0, 0)),
        ],
        out_specs=pl.BlockSpec((128 * CAP, D), lambda i: (0, 0)),
        scratch_shapes=[pltpu.VMEM((rows, D), BF16)],
        compiler_params=params(),
    )(slot, tokens, own, other, proj)


def head_source(n):
    head = n >> 6
    column = n & 63
    source = ((head & 3) * RATE + (head >> 2)) * HS + column
    return jnp.where(column < HS, source, -1)


def widen_kernel(q_ref, k_ref, v_ref, out_ref):
    pick = onehot(iota((D, HEADS * HP), 0) == head_source(iota((D, HEADS * HP), 1)))
    for which, ref in enumerate((q_ref, k_ref, v_ref)):
        out_ref[which] = dot(ref[...], pick).astype(BF16)


def widen(q, k, v):
    return pl.pallas_call(
        widen_kernel,
        out_shape=jax.ShapeDtypeStruct((3, D, HEADS * HP), BF16),
        compiler_params=params(),
    )(q, k, v)


def qkv_kernel(place_ref, got_ref, w_ref, near_ref, far_ref):
    block = pl.program_id(0)
    slots_n = got_ref.shape[0]
    pick = onehot(iota((LOC, slots_n), 0) + block * LOC == place_ref[...])
    sequence = dot(pick, got_ref[...]).astype(BF16)
    normed = layer_norm(sequence.astype(F32), 1e-05).astype(BF16)
    for which in range(3):
        acc = dot(normed, w_ref[which])
        if which == 0:
            acc = acc * QSCALE
        if which == 2:
            acc = jnp.where((iota(acc.shape, 1) & 63) == HS, 1.0, acc)
        rows16 = acc.astype(BF16)
        near_ref[which] = rows16
        for j in range(8):
            phase = j >> 1
            far_ref[j, :, which * 128 : which * 128 + 128] = rows16[
                phase * 128 : phase * 128 + 128, j * 128 : j * 128 + 128
            ]


def qkv(place, got, weights):
    slots_n = got.shape[0]
    rows = slots_n // 2
    width = HEADS * HP
    return pl.pallas_call(
        qkv_kernel,
        grid=(rows // LOC,),
        out_shape=(
            jax.ShapeDtypeStruct((3, rows, width), BF16),
            jax.ShapeDtypeStruct((8, rows // RATE, 384), BF16),
        ),
        in_specs=[
            pl.BlockSpec((1, slots_n), lambda i: (0, 0)),
            pl.BlockSpec((slots_n, D), lambda i: (0, 0)),
            pl.BlockSpec((3, D, width), lambda i: (0, 0, 0)),
        ],
        out_specs=(
            pl.BlockSpec((3, LOC, width), lambda i: (0, i, 0)),
            pl.BlockSpec((8, 128, 384), lambda i: (0, i, 0)),
        ),
        compiler_params=params(),
        cost_estimate=pl.CostEstimate(flops=8_000_000_000, bytes_accessed=15_000_000, transcendentals=0),
    )(place, got, weights)


def one_head(q, k, v, head, allowed):
    half = (iota(q.shape, 1) >> 6) == head
    scores = dot_t(jnp.where(half, q, jnp.zeros_like(q)), k)
    scores = jnp.where(allowed, scores, NEG)
    top = jnp.max(scores, axis=-1, keepdims=True)
    weights = jnp.exp2(scores - top).astype(BF16)
    return top, dot(weights, v)


def near_kernel(limit_ref, qkv_ref, out_ref, keep_ref):
    block = pl.program_id(0)
    limit = limit_ref[0] - block * LOC
    r = iota((LOC, LOC), 0)
    c = iota((LOC, LOC), 1)
    position = (c & 127) * RATE + (c >> 7)
    allowed = (position < limit) | (r == c)
    lane = iota((LOC, 128), 1)
    for j in range(8):
        cols = slice(j * 128, j * 128 + 128)
        q, k, v = qkv_ref[0, :, cols], qkv_ref[1, :, cols], qkv_ref[2, :, cols]
        top0, acc0 = one_head(q, k, v, 0, allowed)
        top1, acc1 = one_head(q, k, v, 1, allowed)
        total = jnp.where(lane < HP, acc0[:, HS : HS + 1], acc1[:, HP + HS : HP + HS + 1])
        acc = jnp.where(lane < HP, acc0, acc1)
        out_ref[:, cols] = (acc / total).astype(BF16)
        marked = jnp.where(lane == HS + 1, top0, jnp.where(lane == HP + HS + 1, top1, acc))
        phase = j >> 1
        keep_ref[:, cols] = marked[phase * 128 : phase * 128 + 128]


def near(limit, rows_qkv):
    rows, width = rows_qkv.shape[1:]
    return pl.pallas_call(
        near_kernel,
        grid=(rows // LOC,),
        out_shape=(
            jax.ShapeDtypeStruct((rows, width), BF16),
            jax.ShapeDtypeStruct((rows // RATE, width), F32),
        ),
        in_specs=[
            pl.BlockSpec(memory_space=pltpu.SMEM),
            pl.BlockSpec((3, LOC, width), lambda i: (0, i, 0)),
        ],
        out_specs=(
            pl.BlockSpec((LOC, width), lambda i: (i, 0)),
            pl.BlockSpec((128, width), lambda i: (i, 0)),
        ),
        compiler_params=params(),
        cost_estimate=pl.CostEstimate(
            flops=10_000_000_000, bytes_accessed=12_000_000, transcendentals=rows * LOC * HEADS
        ),
    )(limit, rows_qkv)


def far_kernel(limit_ref, q_ref, kv_ref, out_ref):
    tile = q_ref.shape[0]
    keys = kv_ref.shape[0]
    c = iota((tile, keys), 1)
    r = iota((tile, keys), 0) + pl.program_id(0) * tile
    allowed = (c < limit_ref[0]) | (r == c)
    q = q_ref[:, 0:128]
    k = kv_ref[:, 128:256]
    v = kv_ref[:, 256:384]
    lane = iota((tile, 128), 1)
    top0, acc0 = one_head(q, k, v, 0, allowed)
    top1, acc1 = one_head(q, k, v, 1, allowed)
    low = lane < HP
    total = jnp.where(low, acc0[:, HS : HS + 1], acc1[:, HP + HS : HP + HS + 1])
    acc = jnp.where(low, acc0, acc1)
    level = jnp.where(low, top0, top1) + jnp.log2(total)
    first = level.astype(BF16).astype(F32)
    second = (level - first).astype(BF16).astype(F32)
    third = level - first - second
    spot = lane & 63
    result = jnp.where(
        spot == HS,
        first,
        jnp.where(spot == HS + 1, second, jnp.where(spot == HS + 2, third, acc / total)),
    )
    out_ref[...] = result.astype(BF16)


def far(limit, rows_qkv):
    keys = rows_qkv.shape[0]
    tile = 256
    return pl.pallas_call(
        far_kernel,
        grid=(keys // tile,),
        out_shape=jax.ShapeDtypeStruct((keys, 128), BF16),
        in_specs=[
            pl.BlockSpec(memory_space=pltpu.SMEM),
            pl.BlockSpec((tile, 384), lambda i: (i, 0)),
            pl.BlockSpec((keys, 384), lambda i: (0, 0)),
        ],
        out_specs=pl.BlockSpec((tile, 128), lambda i: (i, 0)),
        compiler_params=params(),
        cost_estimate=pl.CostEstimate(
            flops=10_000_000_000, bytes_accessed=3_000_000, transcendentals=keys * keys * 2
        ),
    )(limit, rows_qkv, rows_qkv)


def merge_kernel(limit_ref, near_ref, keep_ref, far_ref, out_ref, all_ref):
    block = pl.program_id(0)
    limit = limit_ref[0] - block * LOC
    all_ref[...] = near_ref[...]
    low = iota((128, 128), 1) < HP

    def spread(values, at):
        return jnp.where(low, values[:, at : at + 1], values[:, HP + at : HP + at + 1])

    for j in range(8):
        cols = slice(j * 128, j * 128 + 128)
        kept = keep_ref[:, cols]
        came = far_ref[j].astype(F32)
        total = spread(kept, HS)
        top = spread(kept, HS + 1)
        level = spread(came, HS) + spread(came, HS + 1) + spread(came, HS + 2)
        best = jnp.maximum(top, level)
        c_near = jnp.exp2(top - best)
        c_far = jnp.exp2(level - best)
        both = (c_near * kept + c_far * came) / (c_near * total + c_far)
        phase = j >> 1
        all_ref[phase * 128 : phase * 128 + 128, cols] = both.astype(BF16)
    width = HEADS * HP
    narrow = onehot(head_source(iota((D, width), 1)) == iota((D, width), 0))
    packed = dot_t(all_ref[...], narrow).astype(BF16)
    r = iota((LOC, LOC), 0)
    turn = onehot(((r & 3) << 7) + (r >> 2) == iota((LOC, LOC), 1))
    natural = dot(turn, packed)
    live = iota((LOC, D), 0) < limit
    out_ref[...] = jnp.where(live, natural, 0.0).astype(BF16)


def merge(limit, near16, kept, came):
    rows, width = near16.shape
    return pl.pallas_call(
        merge_kernel,
        grid=(rows // LOC,),
        out_shape=jax.ShapeDtypeStruct((rows, D), BF16),
        in_specs=[
            pl.BlockSpec(memory_space=pltpu.SMEM),
            pl.BlockSpec((LOC, width), lambda i: (i, 0)),
            pl.BlockSpec((128, width), lambda i: (i, 0)),
            pl.BlockSpec((8, 128, 128), lambda i: (0, i, 0)),
        ],
        out_specs=pl.BlockSpec((LOC, D), lambda i: (i, 0)),
        scratch_shapes=[pltpu.VMEM((LOC, width), BF16)],
        compiler_params=params(),
    )(limit, near16, kept, came)


def in_place(parts, here):
    stacked = jnp.stack(parts)
    spots = (jnp.arange(SIDE, dtype=jnp.int32) - here) % SIDE
    return jnp.concatenate([lax.dynamic_index_in_dim(stacked, spots[a], 0, False) for a in range(SIDE)])


def shards(
    tile_tokens,
    gate_weight,
    up_weight,
    down_weight,
    proj_weight,
    query_weight,
    key_weight,
    value_weight,
    tile_rank,
    valid_count,
):
    seg_here = lax.axis_index("seg")
    grp_here = lax.axis_index("grp")
    core = grp_here % 2
    x = (grp_here // 8) * 2 + seg_here % 2
    y = seg_here // 2
    z = (grp_here % 8) // 2
    row_count = tile_tokens.shape[0]

    halves = arrange_columns(core.reshape(1), gate_weight, up_weight)
    mate = to_other_core(halves[1])
    mine = halves[0]
    pair = jnp.where(core == 0, jnp.stack([mine, mate]), jnp.stack([mate, mine])).reshape(48, 1024)
    gu = [b.reshape(2, 2, 12, 1024) for b in from_side(pair, 2)]
    gate1 = jnp.concatenate([b[:, 0].reshape(24, 1024) for b in gu])
    up1 = jnp.concatenate([b[:, 1].reshape(24, 1024) for b in gu])
    down1 = in_place(from_side(down_weight, 0), x)
    gate2 = jnp.concatenate(from_side(gate1, 1))
    up2 = jnp.concatenate(from_side(up1, 0))
    down2 = in_place(from_side(down1, 1), y)
    gates, ups, downs = [gate2], [up2], [down2]
    for _ in range(SIDE - 1):
        gates.append(sent(gates[-1], ring_step(0)))
        ups.append(sent(ups[-1], ring_step(1)))
        downs.append(sent(downs[-1], ring_step(2)))
    sign = 1 - 2 * core
    steps = jnp.arange(SIDE, dtype=jnp.int32)
    blocks = jnp.stack([(at - sign * steps) % SIDE for at in (x, y, z)])

    index = jnp.arange(DV, dtype=jnp.int32)
    last = index // 384
    offsets = jnp.where(steps == 3, -1, steps)
    off1 = (index // 24) % SIDE
    off2 = (index // 96) % SIDE
    off1 = jnp.where(off1 == 3, -1, off1)
    off2 = jnp.where(off2 == 3, -1, off2)
    of_core = (index // 12) % 2
    from_z = (z + off1) % SIDE
    order = jnp.stack(
        [
            flat_of(last, (y + off2) % SIDE, from_z, of_core) * 12 + index % 12,
            flat_of((x + off2) % SIDE, last, from_z, of_core) * 12 + index % 12,
        ]
    )
    x_mine = norm_tiles(order, tile_tokens)
    x_mate = to_other_core(x_mine)

    slot, place = slots(tile_rank)
    got_place = lax.all_to_all(place.reshape(128, CAP), ALL, 0, 0, tiled=True)
    wide = widen(query_weight, key_weight, value_weight)

    for_mate = ffn(blocks, x_mate, gates, ups, downs, BF16)
    other = to_other_core(for_mate)
    own = ffn(blocks, x_mine, gates, ups, downs, F32)
    send_rows = tail(slot, tile_tokens, own, other, proj_weight)
    got_rows = lax.all_to_all(send_rows.reshape(128, CAP, D), ALL, 0, 0, tiled=True)

    near_qkv, far_send = qkv(got_place.reshape(1, 128 * CAP), got_rows.reshape(128 * CAP, D), wide)
    far_got = lax.all_to_all(far_send, "seg", 0, 0, tiled=True)
    valid = valid_count[0]
    base = grp_here * (8 * row_count)
    limit = (valid - base - seg_here * row_count).reshape(1)
    near16, kept = near(limit, near_qkv)
    phase = seg_here // 2
    far_limit = ((valid - base - phase + RATE - 1) // RATE).reshape(1)
    far_out = far(far_limit, far_got.reshape(8 * row_count // RATE, 384))
    came = lax.all_to_all(far_out.reshape(8, row_count // RATE, 128), "seg", 0, 0, tiled=True)
    return merge(limit, near16, kept, came)[None]


def solution(mesh):
    return jax.shard_map(
        shards,
        mesh=mesh,
        in_specs=(
            P(("seg", "grp"), None),
            P(("seg", "grp"), None),
            P(("seg", "grp"), None),
            P(("seg", "grp"), None),
            P(),
            P(),
            P(),
            P(),
            P(("seg", "grp")),
            P(),
        ),
        out_specs=P("grp", "seg", None),
        check_vma=False,
    )
```

```python
import math

import jax
import jax.numpy as jnp
from jax import lax
from jax.experimental import pallas as pl
from jax.experimental.pallas import tpu as pltpu
from jax.sharding import PartitionSpec as P
import numpy as np

D = 768
DV = 1536
FF = 2048
HEADS = 16
LOC = 512
RATE = 4
HS = 48
HP = 64
CAP = 16
ALL = ("seg", "grp")
SIDE = 4
REL = (0, 1, 2, 3)
QSCALE = 1.4426950408889634 / math.sqrt(HS)
NEG = -1e30
F32 = jnp.float32
BF16 = jnp.bfloat16
VMEM_BYTES = 56 * 1024 * 1024


def flat_of(x, y, z, core):
    return (y * 2 + x % 2) * 16 + (x // 2) * 8 + z * 2 + core


def device_pairs(move):
    pairs = []
    for x in range(SIDE):
        for y in range(SIDE):
            for z in range(SIDE):
                for core in range(2):
                    there = move(x, y, z, core)
                    there = tuple(v % SIDE for v in there[:3]) + (there[3],)
                    pairs.append((flat_of(x, y, z, core), flat_of(*there)))
    return pairs


def shifted(axis, by):
    def move(x, y, z, core):
        at = [x, y, z]
        at[axis] += by
        return (*at, core)

    return device_pairs(move)


def ring_step(axis):
    def move(x, y, z, core):
        at = [x, y, z]
        at[axis] += 1 - 2 * core
        return (*at, core)

    return device_pairs(move)


def sent(value, pairs):
    return lax.ppermute(value, ALL, pairs)


def to_other_core(value):
    return sent(value, device_pairs(lambda x, y, z, core: (x, y, z, 1 - core)))


def from_side(block, axis):
    return [block if off == 0 else sent(block, shifted(axis, -off)) for off in REL]


def after(value, *others):
    return lax.optimization_barrier((value, *others))[0]


def meta_rows():
    rows = np.zeros((128, 8), np.int32)
    for x in range(SIDE):
        for y in range(SIDE):
            for z in range(SIDE):
                for core in range(2):
                    at = flat_of(x, y, z, core)
                    rows[at, :6] = (core, x, y, z, at // 16, at % 16)
    return rows


SMEM = pl.BlockSpec(memory_space=pltpu.SMEM)


def params(**kw):
    return pltpu.CompilerParams(vmem_limit_bytes=VMEM_BYTES, **kw)


def iota(shape, dim):
    return lax.broadcasted_iota(jnp.int32, shape, dim)


def dot(left, right):
    return jnp.dot(left, right, preferred_element_type=F32)


def dot_t(left, right):
    return lax.dot_general(left, right, (((1,), (1,)), ((), ())), preferred_element_type=F32)


def layer_norm(values, epsilon):
    row_mean = jnp.mean(values, axis=-1, keepdims=True)
    centered = values - row_mean
    row_var = jnp.mean(centered * centered, axis=-1, keepdims=True)
    return centered * lax.rsqrt(row_var + epsilon)


def onehot(mask):
    return jnp.where(mask, 1.0, 0.0).astype(BF16)


def column_kernel(meta_ref, gate_ref, up_ref, mine_ref, other_ref):
    core = meta_ref[0, 0]
    rows = jnp.concatenate([gate_ref[...].astype(F32), up_ref[...].astype(F32)], axis=0).astype(BF16)
    width = 256
    for start in range(0, FF, width):
        n = iota((1, width), 1) + start
        x = (n >> 4) & 3
        y = (n >> 6) & 3
        z = (n >> 8) & 3
        half = (n >> 10) ^ core
        source = ((y * 2 + (x & 1)) * 16 + (x >> 1) * 8 + z * 2 + half) * 16 + (n & 15)
        picked = dot(rows, onehot(iota((FF, width), 0) == source)).astype(BF16)
        out = mine_ref if start < 1024 else other_ref
        out[:, start % 1024 : start % 1024 + width] = picked


def arrange_columns(meta, gate, up):
    return pl.pallas_call(
        column_kernel,
        out_shape=(jax.ShapeDtypeStruct((24, FF // 2), BF16),) * 2,
        in_specs=[SMEM, pl.BlockSpec(memory_space=pltpu.VMEM), pl.BlockSpec(memory_space=pltpu.VMEM)],
        compiler_params=params(),
        cost_estimate=pl.CostEstimate(flops=400_000_000, bytes_accessed=300_000, transcendentals=0),
    )(meta, gate, up)


def pair_kernel(meta_ref, mine_ref, mate_ref, out_ref):
    first = meta_ref[0, 0] == 0
    mine, mate = mine_ref[...].astype(F32), mate_ref[...].astype(F32)
    a = jnp.where(first, mine, mate)
    b = jnp.where(first, mate, mine)
    out_ref[...] = jnp.concatenate([a[:12], b[:12], a[12:], b[12:]], axis=0).astype(BF16)


def pair_rows(meta, mine, mate):
    return pl.pallas_call(
        pair_kernel,
        out_shape=jax.ShapeDtypeStruct((48, FF // 2), BF16),
        in_specs=[SMEM, pl.BlockSpec(memory_space=pltpu.VMEM), pl.BlockSpec(memory_space=pltpu.VMEM)],
        compiler_params=params(),
        cost_estimate=pl.CostEstimate(flops=100_000, bytes_accessed=200_000, transcendentals=0),
    )(meta, mine, mate)


def split_kernel(meta_ref, a_ref, b_ref, c_ref, d_ref, gate_ref, up_ref):
    came = [ref[...].astype(F32) for ref in (a_ref, b_ref, c_ref, d_ref)]
    parts = []
    for at in range(SIDE):
        back = (at - meta_ref[0, 3]) & 3
        part = came[0]
        for number in range(1, SIDE):
            part = jnp.where(back == number, came[number], part)
        parts.append(part)
    gate_ref[...] = jnp.concatenate([p[:24] for p in parts], axis=0).astype(BF16)
    up_ref[...] = jnp.concatenate([p[24:] for p in parts], axis=0).astype(BF16)


def split_rows(meta, parts):
    return pl.pallas_call(
        split_kernel,
        out_shape=(jax.ShapeDtypeStruct((96, FF // 2), BF16),) * 2,
        in_specs=[SMEM] + [pl.BlockSpec(memory_space=pltpu.VMEM)] * 4,
        compiler_params=params(),
        cost_estimate=pl.CostEstimate(flops=100_000, bytes_accessed=800_000, transcendentals=0),
    )(meta, *parts)


def norm_kernel(tokens_ref, out_ref):
    out_ref[...] = layer_norm(tokens_ref[...].astype(F32), 1e-06).astype(BF16)


def norm_tiles(tokens):
    rows = tokens.shape[0]
    tile = 256
    return pl.pallas_call(
        norm_kernel,
        grid=(rows // tile,),
        out_shape=jax.ShapeDtypeStruct((rows, DV), BF16),
        in_specs=[pl.BlockSpec((tile, DV), lambda i: (i, 0))],
        out_specs=pl.BlockSpec((tile, DV), lambda i: (i, 0)),
        compiler_params=params(),
        cost_estimate=pl.CostEstimate(flops=20_000_000, bytes_accessed=6_300_000, transcendentals=0),
    )(tokens)


def ffn_kernel(meta_ref, x_ref, *refs):
    gates, ups, downs = refs[0:4], refs[4:8], refs[8:12]
    out_ref, gate_all, up_all, down_all, hid_ref, sems = refs[12:18]
    first = pl.program_id(0) == 0
    sign = 1 - 2 * meta_ref[0, 0]
    copies = [[], [], []]

    def add(kind, source, target):
        number = sum(len(group) for group in copies)
        copies[kind].append(pltpu.make_async_copy(source, target, sems.at[number]))

    for t in range(SIDE):
        for r in range(SIDE):
            across = (meta_ref[0, 1] - sign * t) & 3
            along = (meta_ref[0, 2] + r) & 3
            spot = along * 4 + (across & 1) * 2 + (across >> 1)
            target = pl.ds(pl.multiple_of(spot * 96, 96), 96)
            add(0, gates[t].at[pl.ds(r * 96, 96)], gate_all.at[target])
            across = (meta_ref[0, 1] + r) & 3
            along = (meta_ref[0, 2] - sign * t) & 3
            spot = along * 4 + (across & 1) * 2 + (across >> 1)
            target = pl.ds(pl.multiple_of(spot * 96, 96), 96)
            add(1, ups[t].at[pl.ds(r * 96, 96)], up_all.at[target])
    for t in range(SIDE):
        block = (meta_ref[0, 3] - sign * t) & 3
        for yr in range(SIDE):
            for xr in range(SIDE):
                spot = block * 16 + ((meta_ref[0, 2] + yr) & 3) * 4 + ((meta_ref[0, 1] + xr) & 3)
                add(
                    2,
                    downs[t].at[pl.ds((yr * 4 + xr) * 16, 16)],
                    down_all.at[pl.ds(pl.multiple_of(spot * 16, 16), 16)],
                )

    @pl.when(first)
    def _():
        for group in copies:
            for copy in group:
                copy.start()

    def settle(kind):
        @pl.when(first)
        def _():
            for copy in copies[kind]:
                copy.wait()

    settle(0)
    settle(1)
    for at in range(0, 1024, 256):
        gate = dot(x_ref[...], gate_all[:, at : at + 256])
        up = dot(x_ref[...], up_all[:, at : at + 256])
        hid_ref[:, at : at + 256] = (gate / (1.0 + jnp.exp(-gate)) * up).astype(BF16)
    settle(2)
    for at in range(0, DV, 512):
        out_ref[:, at : at + 512] = dot(hid_ref[...], down_all[:, at : at + 512]).astype(out_ref.dtype)


def ffn(meta, x, gates, ups, downs, dtype):
    rows = x.shape[0]
    tile = 512
    left = pl.BlockSpec(memory_space=pl.ANY)
    return pl.pallas_call(
        ffn_kernel,
        grid=(rows // tile,),
        out_shape=jax.ShapeDtypeStruct((rows, DV), dtype),
        in_specs=[
            SMEM,
            pl.BlockSpec((tile, DV), lambda i: (i, 0)),
        ]
        + [left] * 12,
        out_specs=pl.BlockSpec((tile, DV), lambda i: (i, 0)),
        scratch_shapes=[
            pltpu.VMEM((DV, 1024), BF16),
            pltpu.VMEM((DV, 1024), BF16),
            pltpu.VMEM((1024, DV), BF16),
            pltpu.VMEM((tile, 1024), BF16),
            pltpu.SemaphoreType.DMA((96,)),
        ],
        compiler_params=params(),
        cost_estimate=pl.CostEstimate(
            flops=2 * rows * DV * 1024 * 3, bytes_accessed=20_000_000, transcendentals=rows * 1024
        ),
    )(meta, x, *gates, *ups, *downs)


def slot_kernel(rank_ref, slot_ref, place_ref):
    rank = rank_ref[...]
    rows = rank.shape[1]
    devices = 128
    target = ((rank & 8191) >> 10) * 16 + (rank >> 13)
    within = rank & 1023
    hit = iota((devices, rows), 0) == target
    marks = onehot(hit)
    earlier = onehot(iota((rows, rows), 0) < iota((rows, rows), 1))
    before = dot(marks, earlier)
    number = jnp.sum(jnp.where(hit, before, 0.0), axis=0, keepdims=True)
    slot = target * CAP + number.astype(jnp.int32)
    slot_ref[...] = slot
    line = iota((8, rows), 0)
    place = ((within >> 9) << 9) + ((within & 3) << 7) + ((within >> 2) & 127)
    values = jnp.where(
        line == 0, place >> 5, jnp.where(line == 1, place & 31, jnp.where(line == 2, 1, 0))
    ).astype(F32).astype(BF16)
    for start in range(0, devices * CAP, 512):
        taken = onehot(iota((512, rows), 0) + start == slot)
        got = dot_t(values, taken)
        coded = got[0:1] * 32.0 + got[1:2] + got[2:3] - 1.0
        place_ref[:, start : start + 512] = coded.astype(jnp.int32)


def slots(rank):
    rows = rank.shape[0]
    return pl.pallas_call(
        slot_kernel,
        out_shape=(
            jax.ShapeDtypeStruct((1, rows), jnp.int32),
            jax.ShapeDtypeStruct((1, 128 * CAP), jnp.int32),
        ),
        compiler_params=params(),
        cost_estimate=pl.CostEstimate(flops=3_000_000_000, bytes_accessed=20_000, transcendentals=0),
    )(rank.reshape(1, rows))


def tail_kernel(slot_ref, tokens_ref, own_ref, other_ref, proj_ref, out_ref, emb_ref):
    step = pl.program_id(0)
    tile = tokens_ref.shape[0]
    rows = emb_ref.shape[0]
    slots_here = out_ref.shape[0]

    @pl.when(step < rows // tile)
    def _():
        mixed = tokens_ref[...].astype(F32) + own_ref[...] + other_ref[...].astype(F32)
        final = layer_norm(mixed, 1e-06).astype(BF16)
        at = pl.ds(pl.multiple_of(step * tile, tile), tile)
        emb_ref[at, :] = dot(final, proj_ref[...]).astype(BF16)

    @pl.when(step >= rows // tile)
    def _():
        start = (step - rows // tile) * slots_here
        pick = onehot(iota((slots_here, rows), 0) == slot_ref[...] - start)
        out_ref[...] = dot(pick, emb_ref[...]).astype(BF16)


def tail(slot, tokens, own, other, proj):
    rows = tokens.shape[0]
    tile = 256
    last = rows // tile - 1
    slots_n = 128 * CAP

    def rows_at(i):
        return (jnp.minimum(i, last), 0)

    return pl.pallas_call(
        tail_kernel,
        grid=(last + 1 + slots_n // 512,),
        out_shape=jax.ShapeDtypeStruct((slots_n, D), BF16),
        in_specs=[
            pl.BlockSpec((1, rows), lambda i: (0, 0)),
            pl.BlockSpec((tile, DV), rows_at),
            pl.BlockSpec((tile, DV), rows_at),
            pl.BlockSpec((tile, DV), rows_at),
            pl.BlockSpec((DV, D), lambda i: (0, 0)),
        ],
        out_specs=pl.BlockSpec((512, D), lambda i: (jnp.maximum(i - last - 1, 0), 0)),
        scratch_shapes=[pltpu.VMEM((rows, D), BF16)],
        compiler_params=params(),
        cost_estimate=pl.CostEstimate(flops=6_000_000_000, bytes_accessed=18_000_000, transcendentals=0),
    )(slot, tokens, own, other, proj)


def head_source(n):
    head = n >> 6
    column = n & 63
    source = ((head & 3) * RATE + (head >> 2)) * HS + column
    return jnp.where(column < HS, source, -1)


def widen_kernel(q_ref, k_ref, v_ref, out_ref):
    pick = onehot(iota((D, HEADS * HP), 0) == head_source(iota((D, HEADS * HP), 1)))
    for which, ref in enumerate((q_ref, k_ref, v_ref)):
        out_ref[which] = dot(ref[...], pick).astype(BF16)


def widen(q, k, v):
    return pl.pallas_call(
        widen_kernel,
        out_shape=jax.ShapeDtypeStruct((3, D, HEADS * HP), BF16),
        compiler_params=params(),
        cost_estimate=pl.CostEstimate(flops=3_600_000_000, bytes_accessed=8_000_000, transcendentals=0),
    )(q, k, v)


def three_rows(normed, w_ref, cols):
    result = []
    for which in range(3):
        acc = dot(normed, w_ref[which, :, cols])
        if which == 0:
            acc = acc * QSCALE
        if which == 2:
            acc = jnp.where((iota(acc.shape, 1) & 63) == HS, 1.0, acc)
        result.append(acc.astype(BF16))
    return result


def place_kernel(place_ref, got_ref, w_ref, normed_ref, far_ref):
    block = pl.program_id(0)
    slots_n = got_ref.shape[0]
    pick = onehot(iota((LOC, slots_n), 0) + block * LOC == place_ref[...])
    sequence = dot(pick, got_ref[...]).astype(BF16)
    normed = layer_norm(sequence.astype(F32), 1e-05).astype(BF16)
    normed_ref[...] = normed
    for phase in range(RATE):
        part = normed[phase * 128 : phase * 128 + 128]
        qkv = three_rows(part, w_ref, slice(phase * 256, phase * 256 + 256))
        for which in range(3):
            for i in range(2):
                far_ref[2 * phase + i, :, which * 128 : which * 128 + 128] = qkv[which][
                    :, i * 128 : i * 128 + 128
                ]


def place_rows(place, got, weights):
    slots_n = got.shape[0]
    rows = slots_n // 2
    width = HEADS * HP
    return pl.pallas_call(
        place_kernel,
        grid=(rows // LOC,),
        out_shape=(
            jax.ShapeDtypeStruct((rows, D), BF16),
            jax.ShapeDtypeStruct((8, rows // RATE, 384), BF16),
        ),
        in_specs=[
            pl.BlockSpec((1, slots_n), lambda i: (0, 0)),
            pl.BlockSpec((slots_n, D), lambda i: (0, 0)),
            pl.BlockSpec((3, D, width), lambda i: (0, 0, 0)),
        ],
        out_specs=(
            pl.BlockSpec((LOC, D), lambda i: (i, 0)),
            pl.BlockSpec((8, 128, 384), lambda i: (0, i, 0)),
        ),
        compiler_params=params(),
        cost_estimate=pl.CostEstimate(flops=4_000_000_000, bytes_accessed=11_000_000, transcendentals=0),
    )(place, got, weights)


def near_limit(meta_ref, valid_ref):
    return valid_ref[0] - meta_ref[0, 5] * (8 * 1024) - meta_ref[0, 4] * 1024


def head_queries(q, head):
    return jnp.where((iota(q.shape, 1) >> 6) == head, q, jnp.zeros_like(q))


def weigh(scores, v):
    top = jnp.max(scores, axis=-1, keepdims=True)
    weights = jnp.exp2(scores - top).astype(BF16)
    return top, dot(weights, v)


def near_kernel(meta_ref, valid_ref, normed_ref, w_ref, out_ref, keep_ref, bias_ref):
    block = pl.program_id(0)
    limit = near_limit(meta_ref, valid_ref) - block * LOC
    r = iota((LOC, LOC), 0)
    c = iota((LOC, LOC), 1)
    position = (c & 127) * RATE + (c >> 7)
    bias_ref[...] = jnp.where((position < limit) | (r == c), 0.0, NEG)
    normed = normed_ref[...]
    lane = iota((LOC, 128), 1)
    for j in range(8):
        cols = slice(j * 128, j * 128 + 128)
        if j % 2 == 0:
            two = three_rows(normed, w_ref, slice(j * 128, j * 128 + 256))
        q, k, v = [rows16[:, j % 2 * 128 : j % 2 * 128 + 128] for rows16 in two]
        scores = [dot_t(head_queries(q, head), k) for head in range(2)]
        top0, acc0 = weigh(scores[0] + bias_ref[...], v)
        top1, acc1 = weigh(scores[1] + bias_ref[...], v)
        total = jnp.where(lane < HP, acc0[:, HS : HS + 1], acc1[:, HP + HS : HP + HS + 1])
        acc = jnp.where(lane < HP, acc0, acc1)
        out_ref[:, cols] = (acc / total).astype(BF16)
        marked = jnp.where(lane == HS + 1, top0, jnp.where(lane == HP + HS + 1, top1, acc))
        phase = j >> 1
        keep_ref[:, cols] = marked[phase * 128 : phase * 128 + 128]


def near(meta, valid, normed, weights):
    rows = normed.shape[0]
    width = HEADS * HP
    return pl.pallas_call(
        near_kernel,
        grid=(rows // LOC,),
        out_shape=(
            jax.ShapeDtypeStruct((rows, width), BF16),
            jax.ShapeDtypeStruct((rows // RATE, width), F32),
        ),
        in_specs=[
            SMEM,
            SMEM,
            pl.BlockSpec((LOC, D), lambda i: (i, 0)),
            pl.BlockSpec((3, D, width), lambda i: (0, 0, 0)),
        ],
        out_specs=(
            pl.BlockSpec((LOC, width), lambda i: (i, 0)),
            pl.BlockSpec((128, width), lambda i: (i, 0)),
        ),
        scratch_shapes=[pltpu.VMEM((LOC, LOC), F32)],
        compiler_params=params(),
        cost_estimate=pl.CostEstimate(
            flops=15_000_000_000, bytes_accessed=12_000_000, transcendentals=rows * LOC * HEADS
        ),
    )(meta, valid, normed, weights)


def far_kernel(meta_ref, valid_ref, q_ref, kv_ref, out_ref, score_ref):
    tile = q_ref.shape[0]
    keys = kv_ref.shape[0]
    limit = (valid_ref[0] - meta_ref[0, 5] * (8 * 1024) - (meta_ref[0, 4] >> 1) + RATE - 1) >> 2
    bias = jnp.where(iota((1, keys), 1) < limit, 0.0, NEG)
    here = pl.ds(pl.multiple_of(pl.program_id(0) * tile, tile), tile)
    own = iota((tile, tile), 0) == iota((tile, tile), 1)
    k = kv_ref[:, 128:256]
    v = kv_ref[:, 256:384]
    for head in range(2):
        q = head_queries(q_ref[:, 0:128], head)
        score_ref[head] = dot_t(q, k) + bias
        same = dot_t(q, kv_ref[here, 128:256])
        score_ref[head, :, here] = jnp.where(own, same, score_ref[head, :, here])
    lane = iota((tile, 128), 1)
    top0, acc0 = weigh(score_ref[0], v)
    top1, acc1 = weigh(score_ref[1], v)
    low = lane < HP
    total = jnp.where(low, acc0[:, HS : HS + 1], acc1[:, HP + HS : HP + HS + 1])
    acc = jnp.where(low, acc0, acc1)
    level = jnp.where(low, top0, top1) + jnp.log2(total)
    first = level.astype(BF16).astype(F32)
    second = (level - first).astype(BF16).astype(F32)
    third = level - first - second
    spot = lane & 63
    result = jnp.where(
        spot == HS,
        first,
        jnp.where(spot == HS + 1, second, jnp.where(spot == HS + 2, third, acc / total)),
    )
    out_ref[...] = result.astype(BF16)


def far(meta, valid, rows_qkv):
    keys = rows_qkv.shape[0]
    tile = 256
    return pl.pallas_call(
        far_kernel,
        grid=(keys // tile,),
        out_shape=jax.ShapeDtypeStruct((keys, 128), BF16),
        in_specs=[
            SMEM,
            SMEM,
            pl.BlockSpec((tile, 384), lambda i: (i, 0)),
            pl.BlockSpec((keys, 384), lambda i: (0, 0)),
        ],
        out_specs=pl.BlockSpec((tile, 128), lambda i: (i, 0)),
        scratch_shapes=[pltpu.VMEM((2, tile, keys), F32)],
        compiler_params=params(),
        cost_estimate=pl.CostEstimate(
            flops=10_000_000_000, bytes_accessed=3_000_000, transcendentals=keys * keys * 2
        ),
    )(meta, valid, rows_qkv, rows_qkv)


def merge_kernel(meta_ref, valid_ref, near_ref, keep_ref, far_ref, out_ref, all_ref):
    block = pl.program_id(0)
    limit = near_limit(meta_ref, valid_ref) - block * LOC
    all_ref[...] = near_ref[...]
    low = iota((128, 128), 1) < HP

    def spread(values, at):
        return jnp.where(low, values[:, at : at + 1], values[:, HP + at : HP + at + 1])

    for j in range(8):
        cols = slice(j * 128, j * 128 + 128)
        kept = keep_ref[:, cols]
        came = far_ref[j].astype(F32)
        total = spread(kept, HS)
        top = spread(kept, HS + 1)
        level = spread(came, HS) + spread(came, HS + 1) + spread(came, HS + 2)
        best = jnp.maximum(top, level)
        c_near = jnp.exp2(top - best)
        c_far = jnp.exp2(level - best)
        both = (c_near * kept + c_far * came) / (c_near * total + c_far)
        phase = j >> 1
        all_ref[phase * 128 : phase * 128 + 128, cols] = both.astype(BF16)
    width = HEADS * HP
    narrow = onehot(head_source(iota((D, width), 1)) == iota((D, width), 0))
    packed = dot_t(all_ref[...], narrow).astype(BF16)
    r = iota((LOC, LOC), 0)
    turn = onehot(((r & 3) << 7) + (r >> 2) == iota((LOC, LOC), 1))
    natural = dot(turn, packed)
    live = iota((LOC, D), 0) < limit
    out_ref[...] = jnp.where(live, natural, 0.0).astype(BF16)


def merge(meta, valid, near16, kept, came):
    rows, width = near16.shape
    return pl.pallas_call(
        merge_kernel,
        grid=(rows // LOC,),
        out_shape=jax.ShapeDtypeStruct((rows, D), BF16),
        in_specs=[
            SMEM,
            SMEM,
            pl.BlockSpec((LOC, width), lambda i: (i, 0)),
            pl.BlockSpec((128, width), lambda i: (i, 0)),
            pl.BlockSpec((8, 128, 128), lambda i: (0, i, 0)),
        ],
        out_specs=pl.BlockSpec((LOC, D), lambda i: (i, 0)),
        scratch_shapes=[pltpu.VMEM((LOC, width), BF16)],
        compiler_params=params(),
    )(meta, valid, near16, kept, came)


def shards(
    tile_tokens,
    gate_weight,
    up_weight,
    down_weight,
    proj_weight,
    query_weight,
    key_weight,
    value_weight,
    tile_rank,
    valid_count,
):
    row_count = tile_tokens.shape[0]
    me = lax.axis_index(ALL)
    meta = lax.dynamic_slice(jnp.asarray(meta_rows()), (me, 0), (1, 8))

    mine, others = arrange_columns(meta, gate_weight, up_weight)
    down1 = jnp.concatenate(from_side(down_weight, 0))
    pair = pair_rows(meta, mine, to_other_core(others))
    pair, down1 = lax.optimization_barrier((pair, down1))
    gate1, up1 = split_rows(meta, from_side(pair, 2))
    down2 = jnp.concatenate(from_side(down1, 1))
    gate2 = jnp.concatenate(from_side(gate1, 1))
    up2 = jnp.concatenate(from_side(up1, 0))
    gates, ups, downs = [gate2], [up2], [down2]

    def one_round():
        gates.append(sent(gates[-1], ring_step(0)))
        ups.append(sent(ups[-1], ring_step(1)))
        downs.append(sent(downs[-1], ring_step(2)))

    def hold(*others):
        held = lax.optimization_barrier((gates[-1], ups[-1], downs[-1], *others))
        gates[-1], ups[-1], downs[-1] = held[:3]
        return held[3:]

    tokens, rank = hold(tile_tokens, tile_rank)
    one_round()
    x = norm_tiles(tokens)
    slot, place = slots(rank)
    x, place = hold(x, place)
    one_round()
    x_mate = to_other_core(x)
    got_place = lax.all_to_all(place.reshape(128, CAP), ALL, 0, 0, tiled=True)
    one_round()
    x_mate = after(x_mate, got_place)
    wide = widen(query_weight, key_weight, value_weight)

    for_mate = ffn(meta, x_mate, gates, ups, downs, BF16)
    other = to_other_core(for_mate)
    own = ffn(meta, x, gates, ups, downs, F32)
    send_rows = tail(slot, tile_tokens, own, other, proj_weight)
    got_rows = lax.all_to_all(send_rows.reshape(128, CAP, D), ALL, 0, 0, tiled=True)

    normed, far_send = place_rows(
        got_place.reshape(1, 128 * CAP), got_rows.reshape(128 * CAP, D), wide
    )
    far_got = lax.all_to_all(far_send, "seg", 0, 0, tiled=True)
    near16, kept = near(meta, valid_count, normed, wide)
    far_got = after(far_got, near16)
    far_out = far(meta, valid_count, far_got.reshape(8 * row_count // RATE, 384))
    came = lax.all_to_all(far_out.reshape(8, row_count // RATE, 128), "seg", 0, 0, tiled=True)
    return merge(meta, valid_count, near16, kept, came)[None]


def solution(mesh):
    return jax.shard_map(
        shards,
        mesh=mesh,
        in_specs=(
            P(("seg", "grp"), None),
            P(("seg", "grp"), None),
            P(("seg", "grp"), None),
            P(("seg", "grp"), None),
            P(),
            P(),
            P(),
            P(),
            P(("seg", "grp")),
            P(),
        ),
        out_specs=P("grp", "seg", None),
        check_vma=False,
    )
```

```python
import math

import jax
import jax.numpy as jnp
from jax import lax
from jax.experimental import pallas as pl
from jax.experimental.pallas import tpu as pltpu
from jax.sharding import PartitionSpec as P
import numpy as np

D = 768
DV = 1536
FF = 2048
HEADS = 16
LOC = 512
RATE = 4
HS = 48
HP = 64
CAP = 16
ALL = ("seg", "grp")
SIDE = 4
REL = (0, 1, 2, 3)
QSCALE = 1.4426950408889634 / math.sqrt(HS)
NEG = -1e30
F32 = jnp.float32
BF16 = jnp.bfloat16
VMEM_BYTES = 56 * 1024 * 1024


def flat_of(x, y, z, core):
    return (y * 2 + x % 2) * 16 + (x // 2) * 8 + z * 2 + core


def device_pairs(move):
    pairs = []
    for x in range(SIDE):
        for y in range(SIDE):
            for z in range(SIDE):
                for core in range(2):
                    there = move(x, y, z, core)
                    there = tuple(v % SIDE for v in there[:3]) + (there[3],)
                    pairs.append((flat_of(x, y, z, core), flat_of(*there)))
    return pairs


def shifted(axis, by):
    def move(x, y, z, core):
        at = [x, y, z]
        at[axis] += by
        return (*at, core)

    return device_pairs(move)


def ring_step(axis):
    def move(x, y, z, core):
        at = [x, y, z]
        at[axis] += 1 - 2 * core
        return (*at, core)

    return device_pairs(move)


def sent(value, pairs):
    return lax.ppermute(value, ALL, pairs)


def to_other_core(value):
    return sent(value, device_pairs(lambda x, y, z, core: (x, y, z, 1 - core)))


def from_side(block, axis):
    return [block if off == 0 else sent(block, shifted(axis, -off)) for off in REL]


def after(value, *others):
    return lax.optimization_barrier((value, *others))[0]


def meta_rows():
    rows = np.zeros((128, 8), np.int32)
    for x in range(SIDE):
        for y in range(SIDE):
            for z in range(SIDE):
                for core in range(2):
                    at = flat_of(x, y, z, core)
                    rows[at, :6] = (core, x, y, z, at // 16, at % 16)
    return rows


SMEM = pl.BlockSpec(memory_space=pltpu.SMEM)


def params(**kw):
    return pltpu.CompilerParams(vmem_limit_bytes=VMEM_BYTES, **kw)


def iota(shape, dim):
    return lax.broadcasted_iota(jnp.int32, shape, dim)


def dot(left, right):
    return jnp.dot(left, right, preferred_element_type=F32)


def dot_t(left, right):
    return lax.dot_general(left, right, (((1,), (1,)), ((), ())), preferred_element_type=F32)


def layer_norm(values, epsilon):
    row_mean = jnp.mean(values, axis=-1, keepdims=True)
    centered = values - row_mean
    row_var = jnp.mean(centered * centered, axis=-1, keepdims=True)
    return centered * lax.rsqrt(row_var + epsilon)


def onehot(mask):
    return jnp.where(mask, 1.0, 0.0).astype(BF16)


def column_kernel(meta_ref, gate_ref, up_ref, mine_ref, other_ref):
    core = meta_ref[0, 0]
    rows = jnp.concatenate([gate_ref[...].astype(F32), up_ref[...].astype(F32)], axis=0).astype(BF16)
    width = 256
    for start in range(0, FF, width):
        n = iota((1, width), 1) + start
        x = (n >> 4) & 3
        y = (n >> 6) & 3
        z = (n >> 8) & 3
        half = (n >> 10) ^ core
        source = ((y * 2 + (x & 1)) * 16 + (x >> 1) * 8 + z * 2 + half) * 16 + (n & 15)
        picked = dot(rows, onehot(iota((FF, width), 0) == source)).astype(BF16)
        out = mine_ref if start < 1024 else other_ref
        out[:, start % 1024 : start % 1024 + width] = picked


def arrange_columns(meta, gate, up):
    return pl.pallas_call(
        column_kernel,
        out_shape=(jax.ShapeDtypeStruct((24, FF // 2), BF16),) * 2,
        in_specs=[SMEM, pl.BlockSpec(memory_space=pltpu.VMEM), pl.BlockSpec(memory_space=pltpu.VMEM)],
        compiler_params=params(),
        cost_estimate=pl.CostEstimate(flops=400_000_000, bytes_accessed=300_000, transcendentals=0),
    )(meta, gate, up)


def pair_kernel(meta_ref, mine_ref, mate_ref, out_ref):
    first = meta_ref[0, 0] == 0
    mine, mate = mine_ref[...].astype(F32), mate_ref[...].astype(F32)
    a = jnp.where(first, mine, mate)
    b = jnp.where(first, mate, mine)
    out_ref[...] = jnp.concatenate([a[:12], b[:12], a[12:], b[12:]], axis=0).astype(BF16)


def pair_rows(meta, mine, mate):
    return pl.pallas_call(
        pair_kernel,
        out_shape=jax.ShapeDtypeStruct((48, FF // 2), BF16),
        in_specs=[SMEM, pl.BlockSpec(memory_space=pltpu.VMEM), pl.BlockSpec(memory_space=pltpu.VMEM)],
        compiler_params=params(),
        cost_estimate=pl.CostEstimate(flops=100_000, bytes_accessed=200_000, transcendentals=0),
    )(meta, mine, mate)


def in_order(came, here):
    parts = []
    for at in range(SIDE):
        back = (at - here) & 3
        part = came[0]
        for number in range(1, SIDE):
            part = jnp.where(back == number, came[number], part)
        parts.append(part)
    return parts


def stack_kernel(meta_ref, a_ref, b_ref, c_ref, d_ref, out_ref):
    came = [ref[...].astype(F32) for ref in (a_ref, b_ref, c_ref, d_ref)]
    out_ref[...] = jnp.concatenate(in_order(came, meta_ref[0, 1]), axis=0).astype(BF16)


def stack_down(meta, parts):
    rows, width = parts[0].shape
    return pl.pallas_call(
        stack_kernel,
        out_shape=jax.ShapeDtypeStruct((SIDE * rows, width), BF16),
        in_specs=[SMEM] + [pl.BlockSpec(memory_space=pltpu.VMEM)] * 4,
        compiler_params=params(),
        cost_estimate=pl.CostEstimate(flops=100_000, bytes_accessed=400_000, transcendentals=0),
    )(meta, *parts)


def split_kernel(meta_ref, a_ref, b_ref, c_ref, d_ref, gate_ref, up_ref):
    came = [ref[...].astype(F32) for ref in (a_ref, b_ref, c_ref, d_ref)]
    parts = in_order(came, meta_ref[0, 3])
    gate_ref[...] = jnp.concatenate([p[:24] for p in parts], axis=0).astype(BF16)
    up_ref[...] = jnp.concatenate([p[24:] for p in parts], axis=0).astype(BF16)


def split_rows(meta, parts):
    return pl.pallas_call(
        split_kernel,
        out_shape=(jax.ShapeDtypeStruct((96, FF // 2), BF16),) * 2,
        in_specs=[SMEM] + [pl.BlockSpec(memory_space=pltpu.VMEM)] * 4,
        compiler_params=params(),
        cost_estimate=pl.CostEstimate(flops=100_000, bytes_accessed=800_000, transcendentals=0),
    )(meta, *parts)


def norm_kernel(tokens_ref, out_ref):
    out_ref[...] = layer_norm(tokens_ref[...].astype(F32), 1e-06).astype(BF16)


def norm_tiles(tokens):
    rows = tokens.shape[0]
    tile = 256
    return pl.pallas_call(
        norm_kernel,
        grid=(rows // tile,),
        out_shape=jax.ShapeDtypeStruct((rows, DV), BF16),
        in_specs=[pl.BlockSpec((tile, DV), lambda i: (i, 0))],
        out_specs=pl.BlockSpec((tile, DV), lambda i: (i, 0)),
        compiler_params=params(),
        cost_estimate=pl.CostEstimate(flops=20_000_000, bytes_accessed=6_300_000, transcendentals=0),
    )(tokens)


def ffn_kernel(meta_ref, x_ref, *refs):
    gates, ups, downs = refs[0:4], refs[4:8], refs[8:12]
    out_ref, gate_out, up_out, down_out, gate_all, up_all, down_all, hid_ref, sems, out_sems = refs[13:23]
    first = pl.program_id(0) == 0
    sign = 1 - 2 * meta_ref[0, 0]
    copies = [[], [], []]

    def add(kind, source, target):
        number = sum(len(group) for group in copies)
        copies[kind].append(pltpu.make_async_copy(source, target, sems.at[number]))

    for t in range(SIDE):
        for r in range(SIDE):
            across = (meta_ref[0, 1] - sign * t) & 3
            along = (meta_ref[0, 2] + r) & 3
            spot = along * 4 + (across & 1) * 2 + (across >> 1)
            target = pl.ds(pl.multiple_of(spot * 96, 96), 96)
            add(0, gates[t].at[pl.ds(r * 96, 96)], gate_all.at[target])
            across = (meta_ref[0, 1] + r) & 3
            along = (meta_ref[0, 2] - sign * t) & 3
            spot = along * 4 + (across & 1) * 2 + (across >> 1)
            target = pl.ds(pl.multiple_of(spot * 96, 96), 96)
            add(1, ups[t].at[pl.ds(r * 96, 96)], up_all.at[target])
    for t in range(SIDE):
        block = (meta_ref[0, 3] - sign * t) & 3
        for yr in range(SIDE):
            spot = block * 4 + ((meta_ref[0, 2] + yr) & 3)
            add(
                2,
                downs[t].at[pl.ds(yr * 64, 64)],
                down_all.at[pl.ds(pl.multiple_of(spot * 64, 64), 64)],
            )

    @pl.when(first)
    def _():
        for group in copies:
            for copy in group:
                copy.start()

    def settle(kind):
        @pl.when(first)
        def _():
            for copy in copies[kind]:
                copy.wait()

    settle(0)
    settle(1)
    settle(2)
    kept = [
        pltpu.make_async_copy(whole, out, out_sems.at[number])
        for number, (whole, out) in enumerate(
            ((gate_all, gate_out), (up_all, up_out), (down_all, down_out))
        )
    ]

    @pl.when(first)
    def _():
        for copy in kept:
            copy.start()

    two_products(x_ref, gate_all, up_all, down_all, hid_ref, out_ref)

    @pl.when(pl.program_id(0) == pl.num_programs(0) - 1)
    def _():
        for copy in kept:
            copy.wait()


def two_products(x_ref, gate_all, up_all, down_all, hid_ref, out_ref):
    for at in range(0, 1024, 256):
        gate = dot(x_ref[...], gate_all[:, at : at + 256])
        up = dot(x_ref[...], up_all[:, at : at + 256])
        hid_ref[:, at : at + 256] = (gate / (1.0 + jnp.exp(-gate)) * up).astype(BF16)
    for at in range(0, DV, 512):
        out_ref[:, at : at + 512] = dot(hid_ref[...], down_all[:, at : at + 512]).astype(out_ref.dtype)


def again_kernel(x_ref, gate_all, up_all, down_all, out_ref, hid_ref):
    two_products(x_ref, gate_all, up_all, down_all, hid_ref, out_ref)


def ffn_again(x, gate, up, down):
    rows = x.shape[0]
    tile = 512

    def whole(shape):
        return pl.BlockSpec(shape, lambda i: (0, 0))

    return pl.pallas_call(
        again_kernel,
        grid=(rows // tile,),
        out_shape=jax.ShapeDtypeStruct((rows, DV), BF16),
        in_specs=[pl.BlockSpec((tile, DV), lambda i: (i, 0))]
        + [whole(gate.shape), whole(up.shape), whole(down.shape)],
        out_specs=pl.BlockSpec((tile, DV), lambda i: (i, 0)),
        scratch_shapes=[pltpu.VMEM((tile, 1024), BF16)],
        compiler_params=params(),
        cost_estimate=pl.CostEstimate(
            flops=2 * rows * DV * 1024 * 3, bytes_accessed=20_000_000, transcendentals=rows * 1024
        ),
    )(x, gate, up, down)


def ffn(meta, x, gates, ups, downs, ahead):
    rows = x.shape[0]
    tile = 512
    left = pl.BlockSpec(memory_space=pl.ANY)
    return pl.pallas_call(
        ffn_kernel,
        grid=(rows // tile,),
        out_shape=(
            jax.ShapeDtypeStruct((rows, DV), BF16),
            jax.ShapeDtypeStruct((DV, 1024), BF16),
            jax.ShapeDtypeStruct((DV, 1024), BF16),
            jax.ShapeDtypeStruct((1024, DV), BF16),
        ),
        in_specs=[
            SMEM,
            pl.BlockSpec((tile, DV), lambda i: (i, 0)),
        ]
        + [left] * 13,
        out_specs=(pl.BlockSpec((tile, DV), lambda i: (i, 0)), left, left, left),
        scratch_shapes=[
            pltpu.VMEM((DV, 1024), BF16),
            pltpu.VMEM((DV, 1024), BF16),
            pltpu.VMEM((1024, DV), BF16),
            pltpu.VMEM((tile, 1024), BF16),
            pltpu.SemaphoreType.DMA((48,)),
            pltpu.SemaphoreType.DMA((3,)),
        ],
        compiler_params=params(),
        cost_estimate=pl.CostEstimate(
            flops=2 * rows * DV * 1024 * 3, bytes_accessed=20_000_000, transcendentals=rows * 1024
        ),
    )(meta, x, *gates, *ups, *downs, ahead)


def slot_kernel(rank_ref, slot_ref, place_ref):
    rank = rank_ref[...]
    rows = rank.shape[1]
    devices = 128
    target = ((rank & 8191) >> 10) * 16 + (rank >> 13)
    within = rank & 1023
    hit = iota((devices, rows), 0) == target
    marks = onehot(hit)
    earlier = onehot(iota((rows, rows), 0) < iota((rows, rows), 1))
    before = dot(marks, earlier)
    number = jnp.sum(jnp.where(hit, before, 0.0), axis=0, keepdims=True)
    slot = target * CAP + number.astype(jnp.int32)
    slot_ref[...] = slot
    line = iota((8, rows), 0)
    place = ((within >> 9) << 9) + ((within & 3) << 7) + ((within >> 2) & 127)
    values = jnp.where(
        line == 0, place >> 5, jnp.where(line == 1, place & 31, jnp.where(line == 2, 1, 0))
    ).astype(F32).astype(BF16)
    for start in range(0, devices * CAP, 512):
        taken = onehot(iota((512, rows), 0) + start == slot)
        got = dot_t(values, taken)
        coded = got[0:1] * 32.0 + got[1:2] + got[2:3] - 1.0
        place_ref[:, start : start + 512] = coded.astype(jnp.int32)


def slots(rank):
    rows = rank.shape[0]
    return pl.pallas_call(
        slot_kernel,
        out_shape=(
            jax.ShapeDtypeStruct((1, rows), jnp.int32),
            jax.ShapeDtypeStruct((1, 128 * CAP), jnp.int32),
        ),
        compiler_params=params(),
        cost_estimate=pl.CostEstimate(flops=3_000_000_000, bytes_accessed=20_000, transcendentals=0),
    )(rank.reshape(1, rows))


def tail_kernel(slot_ref, tokens_ref, own_ref, other_ref, proj_ref, out_ref, emb_ref):
    step = pl.program_id(0)
    tile = tokens_ref.shape[0]
    rows = emb_ref.shape[0]
    slots_here = out_ref.shape[0]

    @pl.when(step < rows // tile)
    def _():
        mixed = tokens_ref[...].astype(F32) + own_ref[...].astype(F32) + other_ref[...].astype(F32)
        final = layer_norm(mixed, 1e-06).astype(BF16)
        at = pl.ds(pl.multiple_of(step * tile, tile), tile)
        emb_ref[at, :] = dot(final, proj_ref[...]).astype(BF16)

    @pl.when(step >= rows // tile)
    def _():
        start = (step - rows // tile) * slots_here
        pick = onehot(iota((slots_here, rows), 0) == slot_ref[...] - start)
        out_ref[...] = dot(pick, emb_ref[...]).astype(BF16)


def tail(slot, tokens, own, other, proj):
    rows = tokens.shape[0]
    tile = 256
    last = rows // tile - 1
    slots_n = 128 * CAP

    def rows_at(i):
        return (jnp.minimum(i, last), 0)

    return pl.pallas_call(
        tail_kernel,
        grid=(last + 1 + slots_n // 512,),
        out_shape=jax.ShapeDtypeStruct((slots_n, D), BF16),
        in_specs=[
            pl.BlockSpec((1, rows), lambda i: (0, 0)),
            pl.BlockSpec((tile, DV), rows_at),
            pl.BlockSpec((tile, DV), rows_at),
            pl.BlockSpec((tile, DV), rows_at),
            pl.BlockSpec((DV, D), lambda i: (0, 0)),
        ],
        out_specs=pl.BlockSpec((512, D), lambda i: (jnp.maximum(i - last - 1, 0), 0)),
        scratch_shapes=[pltpu.VMEM((rows, D), BF16)],
        compiler_params=params(),
        cost_estimate=pl.CostEstimate(flops=6_000_000_000, bytes_accessed=18_000_000, transcendentals=0),
    )(slot, tokens, own, other, proj)


def head_source(n):
    head = n >> 6
    column = n & 63
    source = ((head & 3) * RATE + (head >> 2)) * HS + column
    return jnp.where(column < HS, source, -1)


def widen_kernel(q_ref, k_ref, v_ref, out_ref):
    pick = onehot(iota((D, HEADS * HP), 0) == head_source(iota((D, HEADS * HP), 1)))
    for which, ref in enumerate((q_ref, k_ref, v_ref)):
        out_ref[which] = dot(ref[...], pick).astype(BF16)


def widen(q, k, v):
    return pl.pallas_call(
        widen_kernel,
        out_shape=jax.ShapeDtypeStruct((3, D, HEADS * HP), BF16),
        compiler_params=params(),
        cost_estimate=pl.CostEstimate(flops=3_600_000_000, bytes_accessed=8_000_000, transcendentals=0),
    )(q, k, v)


def three_rows(normed, w_ref, cols):
    result = []
    for which in range(3):
        acc = dot(normed, w_ref[which, :, cols])
        if which == 0:
            acc = acc * QSCALE
        if which == 2:
            acc = jnp.where((iota(acc.shape, 1) & 63) == HS, 1.0, acc)
        result.append(acc.astype(BF16))
    return result


def place_kernel(place_ref, got_ref, w_ref, normed_ref, far_ref):
    block = pl.program_id(0)
    slots_n = got_ref.shape[0]
    pick = onehot(iota((LOC, slots_n), 0) + block * LOC == place_ref[...])
    sequence = dot(pick, got_ref[...]).astype(BF16)
    normed = layer_norm(sequence.astype(F32), 1e-05).astype(BF16)
    normed_ref[...] = normed
    for phase in range(RATE):
        part = normed[phase * 128 : phase * 128 + 128]
        qkv = three_rows(part, w_ref, slice(phase * 256, phase * 256 + 256))
        for which in range(3):
            for i in range(2):
                far_ref[2 * phase + i, :, which * 128 : which * 128 + 128] = qkv[which][
                    :, i * 128 : i * 128 + 128
                ]


def place_rows(place, got, weights):
    slots_n = got.shape[0]
    rows = slots_n // 2
    width = HEADS * HP
    return pl.pallas_call(
        place_kernel,
        grid=(rows // LOC,),
        out_shape=(
            jax.ShapeDtypeStruct((rows, D), BF16),
            jax.ShapeDtypeStruct((8, rows // RATE, 384), BF16),
        ),
        in_specs=[
            pl.BlockSpec((1, slots_n), lambda i: (0, 0)),
            pl.BlockSpec((slots_n, D), lambda i: (0, 0)),
            pl.BlockSpec((3, D, width), lambda i: (0, 0, 0)),
        ],
        out_specs=(
            pl.BlockSpec((LOC, D), lambda i: (i, 0)),
            pl.BlockSpec((8, 128, 384), lambda i: (0, i, 0)),
        ),
        compiler_params=params(),
        cost_estimate=pl.CostEstimate(flops=4_000_000_000, bytes_accessed=11_000_000, transcendentals=0),
    )(place, got, weights)


def near_limit(meta_ref, valid_ref):
    return valid_ref[0] - meta_ref[0, 5] * (8 * 1024) - meta_ref[0, 4] * 1024


def head_queries(q, head):
    return jnp.where((iota(q.shape, 1) >> 6) == head, q, jnp.zeros_like(q))


def weigh(scores, v):
    top = jnp.max(scores, axis=-1, keepdims=True)
    weights = jnp.exp2(scores - top).astype(BF16)
    return top, dot(weights, v)


def near_kernel(meta_ref, valid_ref, normed_ref, w_ref, out_ref, keep_ref, bias_ref):
    block = pl.program_id(0)
    limit = near_limit(meta_ref, valid_ref) - block * LOC
    r = iota((LOC, LOC), 0)
    c = iota((LOC, LOC), 1)
    position = (c & 127) * RATE + (c >> 7)
    bias_ref[...] = jnp.where((position < limit) | (r == c), 0.0, NEG)
    normed = normed_ref[...]
    lane = iota((LOC, 128), 1)
    for j in range(8):
        cols = slice(j * 128, j * 128 + 128)
        if j % 2 == 0:
            two = three_rows(normed, w_ref, slice(j * 128, j * 128 + 256))
        q, k, v = [rows16[:, j % 2 * 128 : j % 2 * 128 + 128] for rows16 in two]
        scores = [dot_t(head_queries(q, head), k) for head in range(2)]
        top0, acc0 = weigh(scores[0] + bias_ref[...], v)
        top1, acc1 = weigh(scores[1] + bias_ref[...], v)
        total = jnp.where(lane < HP, acc0[:, HS : HS + 1], acc1[:, HP + HS : HP + HS + 1])
        acc = jnp.where(lane < HP, acc0, acc1)
        out_ref[:, cols] = (acc / total).astype(BF16)
        marked = jnp.where(lane == HS + 1, top0, jnp.where(lane == HP + HS + 1, top1, acc))
        phase = j >> 1
        keep_ref[:, cols] = marked[phase * 128 : phase * 128 + 128]


def near(meta, valid, normed, weights):
    rows = normed.shape[0]
    width = HEADS * HP
    return pl.pallas_call(
        near_kernel,
        grid=(rows // LOC,),
        out_shape=(
            jax.ShapeDtypeStruct((rows, width), BF16),
            jax.ShapeDtypeStruct((rows // RATE, width), F32),
        ),
        in_specs=[
            SMEM,
            SMEM,
            pl.BlockSpec((LOC, D), lambda i: (i, 0)),
            pl.BlockSpec((3, D, width), lambda i: (0, 0, 0)),
        ],
        out_specs=(
            pl.BlockSpec((LOC, width), lambda i: (i, 0)),
            pl.BlockSpec((128, width), lambda i: (i, 0)),
        ),
        scratch_shapes=[pltpu.VMEM((LOC, LOC), F32)],
        compiler_params=params(),
        cost_estimate=pl.CostEstimate(
            flops=15_000_000_000, bytes_accessed=12_000_000, transcendentals=rows * LOC * HEADS
        ),
    )(meta, valid, normed, weights)


def far_kernel(meta_ref, valid_ref, q_ref, kv_ref, out_ref, score_ref):
    tile = q_ref.shape[0]
    keys = kv_ref.shape[0]
    limit = (valid_ref[0] - meta_ref[0, 5] * (8 * 1024) - (meta_ref[0, 4] >> 1) + RATE - 1) >> 2
    bias = jnp.where(iota((1, keys), 1) < limit, 0.0, NEG)
    here = pl.ds(pl.multiple_of(pl.program_id(0) * tile, tile), tile)
    own = iota((tile, tile), 0) == iota((tile, tile), 1)
    k = kv_ref[:, 128:256]
    v = kv_ref[:, 256:384]
    for head in range(2):
        q = head_queries(q_ref[:, 0:128], head)
        score_ref[head] = dot_t(q, k) + bias
        same = dot_t(q, kv_ref[here, 128:256])
        score_ref[head, :, here] = jnp.where(own, same, score_ref[head, :, here])
    lane = iota((tile, 128), 1)
    top0, acc0 = weigh(score_ref[0], v)
    top1, acc1 = weigh(score_ref[1], v)
    low = lane < HP
    total = jnp.where(low, acc0[:, HS : HS + 1], acc1[:, HP + HS : HP + HS + 1])
    acc = jnp.where(low, acc0, acc1)
    level = jnp.where(low, top0, top1) + jnp.log2(total)
    first = level.astype(BF16).astype(F32)
    second = (level - first).astype(BF16).astype(F32)
    third = level - first - second
    spot = lane & 63
    result = jnp.where(
        spot == HS,
        first,
        jnp.where(spot == HS + 1, second, jnp.where(spot == HS + 2, third, acc / total)),
    )
    out_ref[...] = result.astype(BF16)


def far(meta, valid, rows_qkv):
    keys = rows_qkv.shape[0]
    tile = 256
    return pl.pallas_call(
        far_kernel,
        grid=(keys // tile,),
        out_shape=jax.ShapeDtypeStruct((keys, 128), BF16),
        in_specs=[
            SMEM,
            SMEM,
            pl.BlockSpec((tile, 384), lambda i: (i, 0)),
            pl.BlockSpec((keys, 384), lambda i: (0, 0)),
        ],
        out_specs=pl.BlockSpec((tile, 128), lambda i: (i, 0)),
        scratch_shapes=[pltpu.VMEM((2, tile, keys), F32)],
        compiler_params=params(),
        cost_estimate=pl.CostEstimate(
            flops=10_000_000_000, bytes_accessed=3_000_000, transcendentals=keys * keys * 2
        ),
    )(meta, valid, rows_qkv, rows_qkv)


def merge_kernel(meta_ref, valid_ref, near_ref, keep_ref, far_ref, out_ref, all_ref):
    block = pl.program_id(0)
    limit = near_limit(meta_ref, valid_ref) - block * LOC
    all_ref[...] = near_ref[...]
    low = iota((128, 128), 1) < HP

    def spread(values, at):
        return jnp.where(low, values[:, at : at + 1], values[:, HP + at : HP + at + 1])

    for j in range(8):
        cols = slice(j * 128, j * 128 + 128)
        kept = keep_ref[:, cols]
        came = far_ref[j].astype(F32)
        total = spread(kept, HS)
        top = spread(kept, HS + 1)
        level = spread(came, HS) + spread(came, HS + 1) + spread(came, HS + 2)
        best = jnp.maximum(top, level)
        c_near = jnp.exp2(top - best)
        c_far = jnp.exp2(level - best)
        both = (c_near * kept + c_far * came) / (c_near * total + c_far)
        phase = j >> 1
        all_ref[phase * 128 : phase * 128 + 128, cols] = both.astype(BF16)
    width = HEADS * HP
    narrow = onehot(head_source(iota((D, width), 1)) == iota((D, width), 0))
    packed = dot_t(all_ref[...], narrow).astype(BF16)
    r = iota((LOC, LOC), 0)
    turn = onehot(((r & 3) << 7) + (r >> 2) == iota((LOC, LOC), 1))
    natural = dot(turn, packed)
    live = iota((LOC, D), 0) < limit
    out_ref[...] = jnp.where(live, natural, 0.0).astype(BF16)


def merge(meta, valid, near16, kept, came):
    rows, width = near16.shape
    return pl.pallas_call(
        merge_kernel,
        grid=(rows // LOC,),
        out_shape=jax.ShapeDtypeStruct((rows, D), BF16),
        in_specs=[
            SMEM,
            SMEM,
            pl.BlockSpec((LOC, width), lambda i: (i, 0)),
            pl.BlockSpec((128, width), lambda i: (i, 0)),
            pl.BlockSpec((8, 128, 128), lambda i: (0, i, 0)),
        ],
        out_specs=pl.BlockSpec((LOC, D), lambda i: (i, 0)),
        scratch_shapes=[pltpu.VMEM((LOC, width), BF16)],
        compiler_params=params(),
    )(meta, valid, near16, kept, came)


def shards(
    tile_tokens,
    gate_weight,
    up_weight,
    down_weight,
    proj_weight,
    query_weight,
    key_weight,
    value_weight,
    tile_rank,
    valid_count,
):
    row_count = tile_tokens.shape[0]
    me = lax.axis_index(ALL)
    meta = lax.dynamic_slice(jnp.asarray(meta_rows()), (me, 0), (1, 8))

    mine, others = arrange_columns(meta, gate_weight, up_weight)
    down1 = stack_down(meta, from_side(down_weight, 0))
    pair = pair_rows(meta, mine, to_other_core(others))
    pair, down1 = lax.optimization_barrier((pair, down1))
    gate1, up1 = split_rows(meta, from_side(pair, 2))
    down2 = jnp.concatenate(from_side(down1, 1))
    gate2 = jnp.concatenate(from_side(gate1, 1))
    up2 = jnp.concatenate(from_side(up1, 0))
    gates, ups, downs = [gate2], [up2], [down2]

    def one_round():
        gates.append(sent(gates[-1], ring_step(0)))
        ups.append(sent(ups[-1], ring_step(1)))
        downs.append(sent(downs[-1], ring_step(2)))

    def hold(*others):
        held = lax.optimization_barrier((gates[-1], ups[-1], downs[-1], *others))
        gates[-1], ups[-1], downs[-1] = held[:3]
        return held[3:]

    tokens, rank = hold(tile_tokens, tile_rank)
    one_round()
    x = norm_tiles(tokens)
    slot, place = slots(rank)
    x, place = hold(x, place)
    one_round()
    x_mate = to_other_core(x)
    got_place = lax.all_to_all(place.reshape(128, CAP), ALL, 0, 0, tiled=True)
    one_round()
    wide = widen(query_weight, key_weight, value_weight)

    for_mate, *weights = ffn(meta, x_mate, gates, ups, downs, got_place)
    other = to_other_core(for_mate)
    own = ffn_again(x, *weights)
    send_rows = tail(slot, tile_tokens, own, other, proj_weight)
    got_rows = lax.all_to_all(send_rows.reshape(128, CAP, D), ALL, 0, 0, tiled=True)

    normed, far_send = place_rows(
        got_place.reshape(1, 128 * CAP), got_rows.reshape(128 * CAP, D), wide
    )
    far_got = lax.all_to_all(far_send, "seg", 0, 0, tiled=True)
    near16, kept = near(meta, valid_count, normed, wide)
    far_got = after(far_got, near16)
    far_out = far(meta, valid_count, far_got.reshape(8 * row_count // RATE, 384))
    came = lax.all_to_all(far_out.reshape(8, row_count // RATE, 128), "seg", 0, 0, tiled=True)
    return merge(meta, valid_count, near16, kept, came)[None]


def solution(mesh):
    return jax.shard_map(
        shards,
        mesh=mesh,
        in_specs=(
            P(("seg", "grp"), None),
            P(("seg", "grp"), None),
            P(("seg", "grp"), None),
            P(("seg", "grp"), None),
            P(),
            P(),
            P(),
            P(),
            P(("seg", "grp")),
            P(),
        ),
        out_specs=P("grp", "seg", None),
        check_vma=False,
    )
```

```python
import math

import jax
import jax.numpy as jnp
from jax import lax
from jax.experimental import pallas as pl
from jax.experimental.pallas import tpu as pltpu
from jax.sharding import PartitionSpec as P
import numpy as np

D = 768
DV = 1536
FF = 2048
HEADS = 16
LOC = 512
RATE = 4
HS = 48
HP = 64
CAP = 16
ALL = ("seg", "grp")
SIDE = 4
REL = (0, 1, 2, 3)
QSCALE = 1.4426950408889634 / math.sqrt(HS)
NEG = -1e30
F32 = jnp.float32
BF16 = jnp.bfloat16
VMEM_BYTES = 56 * 1024 * 1024


def flat_of(x, y, z, core):
    return (y * 2 + x % 2) * 16 + (x // 2) * 8 + z * 2 + core


def device_pairs(move):
    pairs = []
    for x in range(SIDE):
        for y in range(SIDE):
            for z in range(SIDE):
                for core in range(2):
                    there = move(x, y, z, core)
                    there = tuple(v % SIDE for v in there[:3]) + (there[3],)
                    pairs.append((flat_of(x, y, z, core), flat_of(*there)))
    return pairs


def shifted(axis, by):
    def move(x, y, z, core):
        at = [x, y, z]
        at[axis] += by
        return (*at, core)

    return device_pairs(move)


def ring_step(axis):
    def move(x, y, z, core):
        at = [x, y, z]
        at[axis] += 1 - 2 * core
        return (*at, core)

    return device_pairs(move)


def sent(value, pairs):
    return lax.ppermute(value, ALL, pairs)


def to_other_core(value):
    return sent(value, device_pairs(lambda x, y, z, core: (x, y, z, 1 - core)))


def from_side(block, axis):
    return [block if off == 0 else sent(block, shifted(axis, -off)) for off in REL]


def after(value, *others):
    return lax.optimization_barrier((value, *others))[0]


def meta_rows():
    rows = np.zeros((128, 8), np.int32)
    for x in range(SIDE):
        for y in range(SIDE):
            for z in range(SIDE):
                for core in range(2):
                    at = flat_of(x, y, z, core)
                    rows[at, :6] = (core, x, y, z, at // 16, at % 16)
    return rows


SMEM = pl.BlockSpec(memory_space=pltpu.SMEM)


def params(**kw):
    return pltpu.CompilerParams(vmem_limit_bytes=VMEM_BYTES, **kw)


def iota(shape, dim):
    return lax.broadcasted_iota(jnp.int32, shape, dim)


def dot(left, right):
    return jnp.dot(left, right, preferred_element_type=F32)


def dot_t(left, right):
    return lax.dot_general(left, right, (((1,), (1,)), ((), ())), preferred_element_type=F32)


def layer_norm(values, epsilon):
    row_mean = jnp.mean(values, axis=-1, keepdims=True)
    centered = values - row_mean
    row_var = jnp.mean(centered * centered, axis=-1, keepdims=True)
    return centered * lax.rsqrt(row_var + epsilon)


def onehot(mask):
    return jnp.where(mask, 1.0, 0.0).astype(BF16)


def column_kernel(meta_ref, gate_ref, up_ref, mine_ref, other_ref):
    core = meta_ref[0, 0]
    rows = jnp.concatenate([gate_ref[...].astype(F32), up_ref[...].astype(F32)], axis=0).astype(BF16)
    width = 256
    for start in range(0, FF, width):
        n = iota((1, width), 1) + start
        x = (n >> 4) & 3
        y = (n >> 6) & 3
        z = (n >> 8) & 3
        half = (n >> 10) ^ core
        source = ((y * 2 + (x & 1)) * 16 + (x >> 1) * 8 + z * 2 + half) * 16 + (n & 15)
        picked = dot(rows, onehot(iota((FF, width), 0) == source)).astype(BF16)
        out = mine_ref if start < 1024 else other_ref
        out[:, start % 1024 : start % 1024 + width] = picked


def arrange_columns(meta, gate, up):
    return pl.pallas_call(
        column_kernel,
        out_shape=(jax.ShapeDtypeStruct((24, FF // 2), BF16),) * 2,
        in_specs=[SMEM, pl.BlockSpec(memory_space=pltpu.VMEM), pl.BlockSpec(memory_space=pltpu.VMEM)],
        compiler_params=params(),
        cost_estimate=pl.CostEstimate(flops=400_000_000, bytes_accessed=300_000, transcendentals=0),
    )(meta, gate, up)


def pair_kernel(meta_ref, mine_ref, mate_ref, out_ref):
    first = meta_ref[0, 0] == 0
    mine, mate = mine_ref[...].astype(F32), mate_ref[...].astype(F32)
    a = jnp.where(first, mine, mate)
    b = jnp.where(first, mate, mine)
    out_ref[...] = jnp.concatenate([a[:12], b[:12], a[12:], b[12:]], axis=0).astype(BF16)


def pair_rows(meta, mine, mate):
    return pl.pallas_call(
        pair_kernel,
        out_shape=jax.ShapeDtypeStruct((48, FF // 2), BF16),
        in_specs=[SMEM, pl.BlockSpec(memory_space=pltpu.VMEM), pl.BlockSpec(memory_space=pltpu.VMEM)],
        compiler_params=params(),
        cost_estimate=pl.CostEstimate(flops=100_000, bytes_accessed=200_000, transcendentals=0),
    )(meta, mine, mate)


def in_order(came, here):
    parts = []
    for at in range(SIDE):
        back = (at - here) & 3
        part = came[0]
        for number in range(1, SIDE):
            part = jnp.where(back == number, came[number], part)
        parts.append(part)
    return parts


def stack_kernel(meta_ref, a_ref, b_ref, c_ref, d_ref, out_ref):
    came = [ref[...].astype(F32) for ref in (a_ref, b_ref, c_ref, d_ref)]
    out_ref[...] = jnp.concatenate(in_order(came, meta_ref[0, 1]), axis=0).astype(BF16)


def stack_down(meta, parts):
    rows, width = parts[0].shape
    return pl.pallas_call(
        stack_kernel,
        out_shape=jax.ShapeDtypeStruct((SIDE * rows, width), BF16),
        in_specs=[SMEM] + [pl.BlockSpec(memory_space=pltpu.VMEM)] * 4,
        compiler_params=params(),
        cost_estimate=pl.CostEstimate(flops=100_000, bytes_accessed=400_000, transcendentals=0),
    )(meta, *parts)


def split_kernel(meta_ref, a_ref, b_ref, c_ref, d_ref, gate_ref, up_ref):
    came = [ref[...].astype(F32) for ref in (a_ref, b_ref, c_ref, d_ref)]
    parts = in_order(came, meta_ref[0, 3])
    gate_ref[...] = jnp.concatenate([p[:24] for p in parts], axis=0).astype(BF16)
    up_ref[...] = jnp.concatenate([p[24:] for p in parts], axis=0).astype(BF16)


def split_rows(meta, parts):
    return pl.pallas_call(
        split_kernel,
        out_shape=(jax.ShapeDtypeStruct((96, FF // 2), BF16),) * 2,
        in_specs=[SMEM] + [pl.BlockSpec(memory_space=pltpu.VMEM)] * 4,
        compiler_params=params(),
        cost_estimate=pl.CostEstimate(flops=100_000, bytes_accessed=800_000, transcendentals=0),
    )(meta, *parts)


def norm_kernel(tokens_ref, out_ref):
    out_ref[...] = layer_norm(tokens_ref[...].astype(F32), 1e-06).astype(BF16)


def norm_tiles(tokens):
    rows = tokens.shape[0]
    tile = 256
    return pl.pallas_call(
        norm_kernel,
        grid=(rows // tile,),
        out_shape=jax.ShapeDtypeStruct((rows, DV), BF16),
        in_specs=[pl.BlockSpec((tile, DV), lambda i: (i, 0))],
        out_specs=pl.BlockSpec((tile, DV), lambda i: (i, 0)),
        compiler_params=params(),
        cost_estimate=pl.CostEstimate(flops=20_000_000, bytes_accessed=6_300_000, transcendentals=0),
    )(tokens)


def ffn_kernel(meta_ref, x_ref, *refs):
    gates, ups, downs = refs[0:4], refs[4:8], refs[8:12]
    out_ref, gate_out, up_out, down_out, gate_all, up_all, down_all, hid_ref, sems, out_sems = refs[12:22]
    first = pl.program_id(0) == 0
    sign = 1 - 2 * meta_ref[0, 0]
    copies = [[], [], []]

    def add(kind, source, target):
        number = sum(len(group) for group in copies)
        copies[kind].append(pltpu.make_async_copy(source, target, sems.at[number]))

    for t in range(SIDE):
        for r in range(SIDE):
            across = (meta_ref[0, 1] - sign * t) & 3
            along = (meta_ref[0, 2] + r) & 3
            spot = along * 4 + (across & 1) * 2 + (across >> 1)
            target = pl.ds(pl.multiple_of(spot * 96, 96), 96)
            add(0, gates[t].at[pl.ds(r * 96, 96)], gate_all.at[target])
            across = (meta_ref[0, 1] + r) & 3
            along = (meta_ref[0, 2] - sign * t) & 3
            spot = along * 4 + (across & 1) * 2 + (across >> 1)
            target = pl.ds(pl.multiple_of(spot * 96, 96), 96)
            add(1, ups[t].at[pl.ds(r * 96, 96)], up_all.at[target])
    for t in range(SIDE):
        block = (meta_ref[0, 3] - sign * t) & 3
        for yr in range(SIDE):
            spot = block * 4 + ((meta_ref[0, 2] + yr) & 3)
            add(
                2,
                downs[t].at[pl.ds(yr * 64, 64)],
                down_all.at[pl.ds(pl.multiple_of(spot * 64, 64), 64)],
            )

    @pl.when(first)
    def _():
        for group in copies:
            for copy in group:
                copy.start()

    def settle(kind):
        @pl.when(first)
        def _():
            for copy in copies[kind]:
                copy.wait()

    settle(0)
    settle(1)
    settle(2)
    kept = [
        pltpu.make_async_copy(whole, out, out_sems.at[number])
        for number, (whole, out) in enumerate(
            ((gate_all, gate_out), (up_all, up_out), (down_all, down_out))
        )
    ]

    @pl.when(first)
    def _():
        for copy in kept:
            copy.start()

    two_products(x_ref, gate_all, up_all, down_all, hid_ref, out_ref)

    @pl.when(pl.program_id(0) == pl.num_programs(0) - 1)
    def _():
        for copy in kept:
            copy.wait()


def two_products(x_ref, gate_all, up_all, down_all, hid_ref, out_ref):
    for at in range(0, 1024, 256):
        gate = dot(x_ref[...], gate_all[:, at : at + 256])
        up = dot(x_ref[...], up_all[:, at : at + 256])
        hid_ref[:, at : at + 256] = (gate / (1.0 + jnp.exp(-gate)) * up).astype(BF16)
    for at in range(0, DV, 512):
        out_ref[:, at : at + 512] = dot(hid_ref[...], down_all[:, at : at + 512]).astype(out_ref.dtype)


def again_kernel(x_ref, gate_all, up_all, down_all, out_ref, hid_ref):
    two_products(x_ref, gate_all, up_all, down_all, hid_ref, out_ref)


def ffn_again(x, gate, up, down):
    rows = x.shape[0]
    tile = 512

    def whole(shape):
        return pl.BlockSpec(shape, lambda i: (0, 0))

    return pl.pallas_call(
        again_kernel,
        grid=(rows // tile,),
        out_shape=jax.ShapeDtypeStruct((rows, DV), BF16),
        in_specs=[pl.BlockSpec((tile, DV), lambda i: (i, 0))]
        + [whole(gate.shape), whole(up.shape), whole(down.shape)],
        out_specs=pl.BlockSpec((tile, DV), lambda i: (i, 0)),
        scratch_shapes=[pltpu.VMEM((tile, 1024), BF16)],
        compiler_params=params(),
        cost_estimate=pl.CostEstimate(
            flops=2 * rows * DV * 1024 * 3, bytes_accessed=20_000_000, transcendentals=rows * 1024
        ),
    )(x, gate, up, down)


def ffn(meta, x, gates, ups, downs):
    rows = x.shape[0]
    tile = 512
    left = pl.BlockSpec(memory_space=pl.ANY)
    return pl.pallas_call(
        ffn_kernel,
        grid=(rows // tile,),
        out_shape=(
            jax.ShapeDtypeStruct((rows, DV), BF16),
            jax.ShapeDtypeStruct((DV, 1024), BF16),
            jax.ShapeDtypeStruct((DV, 1024), BF16),
            jax.ShapeDtypeStruct((1024, DV), BF16),
        ),
        in_specs=[
            SMEM,
            pl.BlockSpec((tile, DV), lambda i: (i, 0)),
        ]
        + [left] * 12,
        out_specs=(pl.BlockSpec((tile, DV), lambda i: (i, 0)), left, left, left),
        scratch_shapes=[
            pltpu.VMEM((DV, 1024), BF16),
            pltpu.VMEM((DV, 1024), BF16),
            pltpu.VMEM((1024, DV), BF16),
            pltpu.VMEM((tile, 1024), BF16),
            pltpu.SemaphoreType.DMA((48,)),
            pltpu.SemaphoreType.DMA((3,)),
        ],
        compiler_params=params(),
        cost_estimate=pl.CostEstimate(
            flops=2 * rows * DV * 1024 * 3, bytes_accessed=20_000_000, transcendentals=rows * 1024
        ),
    )(meta, x, *gates, *ups, *downs)


def slot_kernel(rank_ref, slot_ref, place_ref):
    rank = rank_ref[...]
    rows = rank.shape[1]
    devices = 128
    target = ((rank & 8191) >> 10) * 16 + (rank >> 13)
    within = rank & 1023
    hit = iota((devices, rows), 0) == target
    marks = onehot(hit)
    earlier = onehot(iota((rows, rows), 0) < iota((rows, rows), 1))
    before = dot(marks, earlier)
    number = jnp.sum(jnp.where(hit, before, 0.0), axis=0, keepdims=True)
    slot = target * CAP + number.astype(jnp.int32)
    slot_ref[...] = slot
    line = iota((8, rows), 0)
    place = ((within >> 9) << 9) + ((within & 3) << 7) + ((within >> 2) & 127)
    values = jnp.where(
        line == 0, place >> 5, jnp.where(line == 1, place & 31, jnp.where(line == 2, 1, 0))
    ).astype(F32).astype(BF16)
    for start in range(0, devices * CAP, 512):
        taken = onehot(iota((512, rows), 0) + start == slot)
        got = dot_t(values, taken)
        coded = got[0:1] * 32.0 + got[1:2] + got[2:3] - 1.0
        place_ref[:, start : start + 512] = coded.astype(jnp.int32)


def slots(rank):
    rows = rank.shape[0]
    return pl.pallas_call(
        slot_kernel,
        out_shape=(
            jax.ShapeDtypeStruct((1, rows), jnp.int32),
            jax.ShapeDtypeStruct((1, 128 * CAP), jnp.int32),
        ),
        compiler_params=params(),
        cost_estimate=pl.CostEstimate(flops=3_000_000_000, bytes_accessed=20_000, transcendentals=0),
    )(rank.reshape(1, rows))


def tail_kernel(slot_ref, tokens_ref, own_ref, other_ref, proj_ref, out_ref, emb_ref):
    step = pl.program_id(0)
    tile = tokens_ref.shape[0]
    rows = emb_ref.shape[0]
    slots_here = out_ref.shape[0]

    @pl.when(step < rows // tile)
    def _():
        mixed = tokens_ref[...].astype(F32) + own_ref[...].astype(F32) + other_ref[...].astype(F32)
        final = layer_norm(mixed, 1e-06).astype(BF16)
        at = pl.ds(pl.multiple_of(step * tile, tile), tile)
        emb_ref[at, :] = dot(final, proj_ref[...]).astype(BF16)

    @pl.when(step >= rows // tile)
    def _():
        start = (step - rows // tile) * slots_here
        pick = onehot(iota((slots_here, rows), 0) == slot_ref[...] - start)
        out_ref[...] = dot(pick, emb_ref[...]).astype(BF16)


def tail(slot, tokens, own, other, proj):
    rows = tokens.shape[0]
    tile = 256
    last = rows // tile - 1
    slots_n = 128 * CAP

    def rows_at(i):
        return (jnp.minimum(i, last), 0)

    return pl.pallas_call(
        tail_kernel,
        grid=(last + 1 + slots_n // 512,),
        out_shape=jax.ShapeDtypeStruct((slots_n, D), BF16),
        in_specs=[
            pl.BlockSpec((1, rows), lambda i: (0, 0)),
            pl.BlockSpec((tile, DV), rows_at),
            pl.BlockSpec((tile, DV), rows_at),
            pl.BlockSpec((tile, DV), rows_at),
            pl.BlockSpec((DV, D), lambda i: (0, 0)),
        ],
        out_specs=pl.BlockSpec((512, D), lambda i: (jnp.maximum(i - last - 1, 0), 0)),
        scratch_shapes=[pltpu.VMEM((rows, D), BF16)],
        compiler_params=params(),
        cost_estimate=pl.CostEstimate(flops=6_000_000_000, bytes_accessed=18_000_000, transcendentals=0),
    )(slot, tokens, own, other, proj)


def head_source(n):
    head = n >> 6
    column = n & 63
    source = ((head & 3) * RATE + (head >> 2)) * HS + column
    return jnp.where(column < HS, source, -1)


def widen_kernel(q_ref, k_ref, v_ref, out_ref):
    pick = onehot(iota((D, HEADS * HP), 0) == head_source(iota((1, HEADS * HP), 1)))
    for which, ref in enumerate((q_ref, k_ref, v_ref)):
        out_ref[which] = dot(ref[...], pick).astype(BF16)


def widen(q, k, v):
    return pl.pallas_call(
        widen_kernel,
        out_shape=jax.ShapeDtypeStruct((3, D, HEADS * HP), BF16),
        compiler_params=params(),
        cost_estimate=pl.CostEstimate(flops=3_600_000_000, bytes_accessed=8_000_000, transcendentals=0),
    )(q, k, v)


def three_rows(normed, w_ref, cols):
    result = []
    for which in range(3):
        acc = dot(normed, w_ref[which, :, cols])
        if which == 0:
            acc = acc * QSCALE
        if which == 2:
            acc = jnp.where((iota(acc.shape, 1) & 63) == HS, 1.0, acc)
        result.append(acc.astype(BF16))
    return result


def place_kernel(place_ref, got_ref, w_ref, normed_ref, far_ref, all_ref):
    block = pl.program_id(0)
    slots_n = got_ref.shape[0]
    pick = onehot(iota((LOC, slots_n), 0) + block * LOC == place_ref[...])
    sequence = dot(pick, got_ref[...]).astype(BF16)
    normed = layer_norm(sequence.astype(F32), 1e-05).astype(BF16)
    normed_ref[...] = normed
    all_ref[pl.ds(pl.multiple_of(block * LOC, LOC), LOC), :] = normed

    @pl.when(block == pl.num_programs(0) - 1)
    def _():
        for phase in range(RATE):
            at = phase * 128
            part = jnp.concatenate([all_ref[at : at + 128], all_ref[LOC + at : LOC + at + 128]])
            qkv = three_rows(part, w_ref, slice(phase * 256, phase * 256 + 256))
            for which in range(3):
                for i in range(2):
                    far_ref[2 * phase + i, :, which * 128 : which * 128 + 128] = qkv[which][
                        :, i * 128 : i * 128 + 128
                    ]


def place_rows(place, got, weights):
    slots_n = got.shape[0]
    rows = slots_n // 2
    width = HEADS * HP
    return pl.pallas_call(
        place_kernel,
        grid=(rows // LOC,),
        out_shape=(
            jax.ShapeDtypeStruct((rows, D), BF16),
            jax.ShapeDtypeStruct((8, rows // RATE, 384), BF16),
        ),
        in_specs=[
            pl.BlockSpec((1, slots_n), lambda i: (0, 0)),
            pl.BlockSpec((slots_n, D), lambda i: (0, 0)),
            pl.BlockSpec((3, D, width), lambda i: (0, 0, 0)),
        ],
        out_specs=(
            pl.BlockSpec((LOC, D), lambda i: (i, 0)),
            pl.BlockSpec((8, rows // RATE, 384), lambda i: (0, 0, 0)),
        ),
        scratch_shapes=[pltpu.VMEM((rows, D), BF16)],
        compiler_params=params(),
        cost_estimate=pl.CostEstimate(flops=4_000_000_000, bytes_accessed=11_000_000, transcendentals=0),
    )(place, got, weights)


def near_limit(meta_ref, valid_ref):
    return valid_ref[0] - meta_ref[0, 5] * (8 * 1024) - meta_ref[0, 4] * 1024


def head_queries(q, head):
    return jnp.where((iota(q.shape, 1) >> 6) == head, q, jnp.zeros_like(q))


def weigh(scores, v):
    top = jnp.max(scores, axis=-1, keepdims=True)
    weights = jnp.exp2(scores - top).astype(BF16)
    return top, dot(weights, v)


def near_kernel(meta_ref, valid_ref, normed_ref, w_ref, out_ref, keep_ref, bias_ref):
    block = pl.program_id(0)
    limit = near_limit(meta_ref, valid_ref) - block * LOC
    r = iota((LOC, LOC), 0)
    c = iota((LOC, LOC), 1)
    position = (c & 127) * RATE + (c >> 7)
    bias_ref[...] = jnp.where((position < limit) | (r == c), 0.0, NEG)
    normed = normed_ref[...]
    lane = iota((LOC, 128), 1)
    for j in range(8):
        cols = slice(j * 128, j * 128 + 128)
        if j % 2 == 0:
            two = three_rows(normed, w_ref, slice(j * 128, j * 128 + 256))
        q, k, v = [rows16[:, j % 2 * 128 : j % 2 * 128 + 128] for rows16 in two]
        scores = [dot_t(head_queries(q, head), k) for head in range(2)]
        top0, acc0 = weigh(scores[0] + bias_ref[...], v)
        top1, acc1 = weigh(scores[1] + bias_ref[...], v)
        total = jnp.where(lane < HP, acc0[:, HS : HS + 1], acc1[:, HP + HS : HP + HS + 1])
        acc = jnp.where(lane < HP, acc0, acc1)
        out_ref[:, cols] = (acc / total).astype(BF16)
        marked = jnp.where(lane == HS + 1, top0, jnp.where(lane == HP + HS + 1, top1, acc))
        phase = j >> 1
        keep_ref[:, cols] = marked[phase * 128 : phase * 128 + 128]


def near(meta, valid, normed, weights):
    rows = normed.shape[0]
    width = HEADS * HP
    return pl.pallas_call(
        near_kernel,
        grid=(rows // LOC,),
        out_shape=(
            jax.ShapeDtypeStruct((rows, width), BF16),
            jax.ShapeDtypeStruct((rows // RATE, width), F32),
        ),
        in_specs=[
            SMEM,
            SMEM,
            pl.BlockSpec((LOC, D), lambda i: (i, 0)),
            pl.BlockSpec((3, D, width), lambda i: (0, 0, 0)),
        ],
        out_specs=(
            pl.BlockSpec((LOC, width), lambda i: (i, 0)),
            pl.BlockSpec((128, width), lambda i: (i, 0)),
        ),
        scratch_shapes=[pltpu.VMEM((LOC, LOC), F32)],
        compiler_params=params(),
        cost_estimate=pl.CostEstimate(
            flops=15_000_000_000, bytes_accessed=12_000_000, transcendentals=rows * LOC * HEADS
        ),
    )(meta, valid, normed, weights)


def far_kernel(meta_ref, valid_ref, q_ref, kv_ref, out_ref, score_ref):
    tile = q_ref.shape[0]
    keys = kv_ref.shape[0]
    limit = (valid_ref[0] - meta_ref[0, 5] * (8 * 1024) - (meta_ref[0, 4] >> 1) + RATE - 1) >> 2
    bias = jnp.where(iota((1, keys), 1) < limit, 0.0, NEG)
    here = pl.ds(pl.multiple_of(pl.program_id(0) * tile, tile), tile)
    own = iota((tile, tile), 0) == iota((tile, tile), 1)
    k = kv_ref[:, 128:256]
    v = kv_ref[:, 256:384]
    for head in range(2):
        q = head_queries(q_ref[:, 0:128], head)
        score_ref[head] = dot_t(q, k) + bias
        same = dot_t(q, kv_ref[here, 128:256])
        score_ref[head, :, here] = jnp.where(own, same, score_ref[head, :, here])
    lane = iota((tile, 128), 1)
    top0, acc0 = weigh(score_ref[0], v)
    top1, acc1 = weigh(score_ref[1], v)
    low = lane < HP
    total = jnp.where(low, acc0[:, HS : HS + 1], acc1[:, HP + HS : HP + HS + 1])
    acc = jnp.where(low, acc0, acc1)
    level = jnp.where(low, top0, top1) + jnp.log2(total)
    first = level.astype(BF16).astype(F32)
    second = (level - first).astype(BF16).astype(F32)
    third = level - first - second
    spot = lane & 63
    result = jnp.where(
        spot == HS,
        first,
        jnp.where(spot == HS + 1, second, jnp.where(spot == HS + 2, third, acc / total)),
    )
    out_ref[...] = result.astype(BF16)


def far(meta, valid, rows_qkv):
    keys = rows_qkv.shape[0]
    tile = 256
    return pl.pallas_call(
        far_kernel,
        grid=(keys // tile,),
        out_shape=jax.ShapeDtypeStruct((keys, 128), BF16),
        in_specs=[
            SMEM,
            SMEM,
            pl.BlockSpec((tile, 384), lambda i: (i, 0)),
            pl.BlockSpec((keys, 384), lambda i: (0, 0)),
        ],
        out_specs=pl.BlockSpec((tile, 128), lambda i: (i, 0)),
        scratch_shapes=[pltpu.VMEM((2, tile, keys), F32)],
        compiler_params=params(),
        cost_estimate=pl.CostEstimate(
            flops=10_000_000_000, bytes_accessed=3_000_000, transcendentals=keys * keys * 2
        ),
    )(meta, valid, rows_qkv, rows_qkv)


def merge_kernel(meta_ref, valid_ref, near_ref, keep_ref, far_ref, out_ref, all_ref):
    block = pl.program_id(0)
    limit = near_limit(meta_ref, valid_ref) - block * LOC
    all_ref[...] = near_ref[...]
    low = iota((128, 128), 1) < HP

    def spread(values, at):
        return jnp.where(low, values[:, at : at + 1], values[:, HP + at : HP + at + 1])

    for j in range(8):
        cols = slice(j * 128, j * 128 + 128)
        kept = keep_ref[:, cols]
        came = far_ref[j].astype(F32)
        total = spread(kept, HS)
        top = spread(kept, HS + 1)
        level = spread(came, HS) + spread(came, HS + 1) + spread(came, HS + 2)
        best = jnp.maximum(top, level)
        c_near = jnp.exp2(top - best)
        c_far = jnp.exp2(level - best)
        both = (c_near * kept + c_far * came) / (c_near * total + c_far)
        phase = j >> 1
        all_ref[phase * 128 : phase * 128 + 128, cols] = both.astype(BF16)
    width = HEADS * HP
    narrow = onehot(head_source(iota((1, width), 1)) == iota((D, width), 0))
    packed = dot_t(all_ref[...], narrow).astype(BF16)
    r = iota((LOC, LOC), 0)
    turn = onehot(((r & 3) << 7) + (r >> 2) == iota((LOC, LOC), 1))
    natural = dot(turn, packed)
    live = iota((LOC, D), 0) < limit
    out_ref[...] = jnp.where(live, natural, 0.0).astype(BF16)


def merge(meta, valid, near16, kept, came):
    rows, width = near16.shape
    return pl.pallas_call(
        merge_kernel,
        grid=(rows // LOC,),
        out_shape=jax.ShapeDtypeStruct((rows, D), BF16),
        in_specs=[
            SMEM,
            SMEM,
            pl.BlockSpec((LOC, width), lambda i: (i, 0)),
            pl.BlockSpec((128, width), lambda i: (i, 0)),
            pl.BlockSpec((8, 128, 128), lambda i: (0, i, 0)),
        ],
        out_specs=pl.BlockSpec((LOC, D), lambda i: (i, 0)),
        scratch_shapes=[pltpu.VMEM((LOC, width), BF16)],
        compiler_params=params(),
    )(meta, valid, near16, kept, came)


def shards(
    tile_tokens,
    gate_weight,
    up_weight,
    down_weight,
    proj_weight,
    query_weight,
    key_weight,
    value_weight,
    tile_rank,
    valid_count,
):
    row_count = tile_tokens.shape[0]
    me = lax.axis_index(ALL)
    meta = lax.dynamic_slice(jnp.asarray(meta_rows()), (me, 0), (1, 8))

    mine, others = arrange_columns(meta, gate_weight, up_weight)
    down1 = stack_down(meta, from_side(down_weight, 0))
    pair = pair_rows(meta, mine, to_other_core(others))
    pair, down1 = lax.optimization_barrier((pair, down1))
    gate1, up1 = split_rows(meta, from_side(pair, 2))
    down2 = jnp.concatenate(from_side(down1, 1))
    gate2 = jnp.concatenate(from_side(gate1, 1))
    up2 = jnp.concatenate(from_side(up1, 0))
    gates, ups, downs = [gate2], [up2], [down2]

    def one_round():
        gates.append(sent(gates[-1], ring_step(0)))
        ups.append(sent(ups[-1], ring_step(1)))
        downs.append(sent(downs[-1], ring_step(2)))

    def hold(*others):
        held = lax.optimization_barrier((gates[-1], ups[-1], downs[-1], *others))
        gates[-1], ups[-1], downs[-1] = held[:3]
        return held[3:]

    tokens, rank = hold(tile_tokens, tile_rank)
    one_round()
    x = norm_tiles(tokens)
    slot, place = slots(rank)
    x, place = hold(x, place)
    one_round()
    x_mate = to_other_core(x)
    got_place = lax.all_to_all(place.reshape(128, CAP), ALL, 0, 0, tiled=True)
    one_round()
    wide = widen(query_weight, key_weight, value_weight)

    for_mate, *weights = ffn(meta, x_mate, gates, ups, downs)
    other = to_other_core(for_mate)
    own = ffn_again(x, *weights)
    send_rows = tail(slot, tile_tokens, own, other, proj_weight)
    got_rows = lax.all_to_all(send_rows.reshape(128, CAP, D), ALL, 0, 0, tiled=True)

    normed, far_send = place_rows(
        got_place.reshape(1, 128 * CAP), got_rows.reshape(128 * CAP, D), wide
    )
    far_got = lax.all_to_all(far_send, "seg", 0, 0, tiled=True)
    near16, kept = near(meta, valid_count, normed, wide)
    far_got = after(far_got, near16)
    far_out = far(meta, valid_count, far_got.reshape(8 * row_count // RATE, 384))
    came = lax.all_to_all(far_out.reshape(8, row_count // RATE, 128), "seg", 0, 0, tiled=True)
    return merge(meta, valid_count, near16, kept, came)[None]


def solution(mesh):
    return jax.shard_map(
        shards,
        mesh=mesh,
        in_specs=(
            P(("seg", "grp"), None),
            P(("seg", "grp"), None),
            P(("seg", "grp"), None),
            P(("seg", "grp"), None),
            P(),
            P(),
            P(),
            P(),
            P(("seg", "grp")),
            P(),
        ),
        out_specs=P("grp", "seg", None),
        check_vma=False,
    )
```
